512 devices in a mesh: ep: 64 (over x, y, core), tp: 8 (over z).
Axes of the slice: x: 4, y: 8, z: 8, core: 2. Of those that a mesh axis runs over, the one named last changes fastest.
Arguments:
- tokens_in: bfloat16 [1024, 3072], P('ep', 'tp'), may hold values from -6 to 6
- d_out: bfloat16 [1024, 3072], P('ep', 'tp'), may hold values from -2.390625 to 2.390625
- gates: float32 [1024, 2], P('ep'), may hold values from 0.2 to 1
- expert_ids: int32 [1024, 2], P('ep'), may hold values from 0 to 7, as said below
- slot_ids: int32 [1024, 2], P('ep'), may hold values from 0 to 5, as said below
- w_gate: bfloat16 [3072, 131072], P(None, ('ep', 'tp')), may hold values from -0.109375 to 0.109375
- w_up: bfloat16 [3072, 131072], P(None, ('ep', 'tp')), may hold values from -0.109375 to 0.109375
- w_down: bfloat16 [131072, 3072], P(('ep', 'tp')), may hold values from -0.046875 to 0.046875
Outputs:
- d_tokens: bfloat16 [1024, 3072], P('ep', 'tp')
- d_gates: float32 [1024, 2], P('ep')
The draws below stay inside these ranges and needn't reach their ends.
Inputs may be any that keep to these rules, and one draw needn't show every extreme that they name: `expert_ids`: the two experts of a token differ. Within each block of tokens b * 16 to (b + 1) * 16 - 1, every expert is named by at most 6 rows, and one and the same expert is named by exactly 6 rows in every block. Rows of one block of 16 tokens that name the same expert have different slot_ids.
All inputs are finite; a program needn't handle non-finite values.
Results may differ from the reference program's by a relative error of at most 0.005.
Values may be sent and summed in bfloat16 or wider, within the bound.
A program may use at most 64 MiB of HBM per device.

```python
import jax
import jax.numpy as jnp
from jax import lax

D = 3072
FF = 16384
EXPERTS = 8
TOK_DEV = 16
CAP = 6
TOKENS = 1024


def route_table(key):
    hot_expert = jax.random.randint(jax.random.fold_in(key, 101), (), 0, EXPERTS).astype(jnp.int32)
    block_keys = jax.random.split(jax.random.fold_in(key, 102), TOKENS // TOK_DEV)
    hot_rows = CAP
    cold_rows = TOK_DEV - CAP
    others_count = EXPERTS - 1

    def slot_order(slot_seed):
        return jax.random.permutation(slot_seed, CAP).astype(jnp.int32)

    def one_block(block_key):
        order_key, offset_key, swap_key, token_key, slot_key = jax.random.split(block_key, 5)
        others = jax.random.permutation(order_key, others_count).astype(jnp.int32)
        others = others + (others >= hot_expert).astype(jnp.int32)
        offset = jax.random.randint(offset_key, (), 0, others_count).astype(jnp.int32)
        hot_counter = jnp.arange(hot_rows, dtype=jnp.int32)
        cold_counter = jnp.arange(cold_rows, dtype=jnp.int32)
        hot_second = others[(hot_counter + offset) % others_count]
        cold_first = others[(hot_rows + 2 * cold_counter + offset) % others_count]
        cold_second = others[(hot_rows + 2 * cold_counter + 1 + offset) % others_count]
        first_column = jnp.concatenate([jnp.zeros((hot_rows,), jnp.int32) + hot_expert, cold_first])
        second_column = jnp.concatenate([hot_second, cold_second])
        paired = jnp.stack([first_column, second_column], axis=1)
        swapped = jax.random.randint(swap_key, (TOK_DEV, 1), 0, 2).astype(jnp.int32)
        paired = jnp.where(swapped == 1, paired[:, ::-1], paired)
        paired = paired[jax.random.permutation(token_key, TOK_DEV)]
        flat_ids = paired.reshape(-1)
        one_hot = (flat_ids[:, None] == jnp.arange(EXPERTS, dtype=jnp.int32)[None, :]).astype(jnp.int32)
        rank_values = jnp.sum((jnp.cumsum(one_hot, axis=0) - 1) * one_hot, axis=1)
        slot_orders = jax.vmap(slot_order)(jax.random.split(slot_key, EXPERTS))
        slot_values = slot_orders[flat_ids, rank_values]
        return (paired, slot_values.reshape(TOK_DEV, 2))
    chosen_ids, slot_values = jax.vmap(one_block)(block_keys)
    return (chosen_ids.reshape(TOKENS, 2).astype(jnp.int32), slot_values.reshape(TOKENS, 2).astype(jnp.int32))


def draw_expert_ids(key, part):
    shared = route_table(key)
    return shared[0]


def draw_slot_ids(key, part):
    shared = route_table(key)
    return shared[1]


def levels(own_key, extent, shards, smallest, largest):
    factor_of, own = 1.0, jax.random.fold_in(own_key, 6)
    for axis_at, parts in shards:
        steps = jnp.exp(jax.random.uniform(jax.random.fold_in(own, axis_at), (parts,), jnp.float32, smallest / len(shards), largest / len(shards)))
        factor_of = factor_of * jnp.repeat(steps, extent[axis_at] // parts).reshape([-1 if axis == axis_at else 1 for axis in range(len(extent))])
    return factor_of


def gaussian(rng, extent, deviation, most, cuts=(), held_as=jnp.bfloat16):
    drawn = deviation * jax.random.normal(rng, extent, jnp.float32)
    if cuts:
        drawn = drawn * levels(rng, extent, cuts, -0.22, 0.18)
    return jnp.clip(drawn, -most, most).astype(held_as)


def setup_inputs(seed: int = 0) -> dict:
    splits = jax.random.split(jax.random.key(seed), 9)
    tokens_in = gaussian(splits[0], (TOKENS, D), 1.0, 6.0, ((0, 64), (1, 8)))
    d_out = gaussian(splits[1], (TOKENS, D), 0.3, 2.390625, ((0, 64), (1, 8)))
    gates = jnp.clip(0.2 + 0.8 * jax.random.uniform(splits[2], (TOKENS, 2), jnp.float32) ** levels(splits[2], (TOKENS, 2), ((0, 64),), -0.2, 0.2), 0.2, 1.0)
    expert_ids = draw_expert_ids(jax.random.fold_in(splits[8], 71), 0)
    slot_ids = draw_slot_ids(jax.random.fold_in(splits[8], 71), 0)
    w_gate = gaussian(splits[5], (D, EXPERTS * FF), D ** -0.5, 0.109375, ((1, 512),))
    w_up = gaussian(splits[6], (D, EXPERTS * FF), D ** -0.5, 0.109375, ((1, 512),))
    w_down = gaussian(splits[7], (EXPERTS * FF, D), FF ** -0.5, 0.046875, ((0, 512),))
    return dict(tokens_in=tokens_in, d_out=d_out, gates=gates, expert_ids=expert_ids, slot_ids=slot_ids, w_gate=w_gate, w_up=w_up, w_down=w_down)


def expert_pass(expert, rows_in, rows_back, w_gate, w_up, w_down):
    gate_cols = lax.dynamic_slice_in_dim(w_gate, expert * FF, FF, 1)
    up_cols = lax.dynamic_slice_in_dim(w_up, expert * FF, FF, 1)
    down_rows = lax.dynamic_slice_in_dim(w_down, expert * FF, FF, 0)
    gate_pre = jnp.dot(rows_in, gate_cols, preferred_element_type=jnp.float32)
    up_pre = jnp.dot(rows_in, up_cols, preferred_element_type=jnp.float32)
    back_grad = jnp.dot(rows_back, down_rows.T, preferred_element_type=jnp.float32)
    sigmoid_gate = jax.nn.sigmoid(gate_pre)
    silu_gate = gate_pre * sigmoid_gate
    scores = jnp.sum(silu_gate * up_pre * back_grad, axis=1)
    grad_gate = (back_grad * up_pre * sigmoid_gate * (1.0 + gate_pre * (1.0 - sigmoid_gate))).astype(jnp.bfloat16)
    grad_up = (back_grad * silu_gate).astype(jnp.bfloat16)
    row_grad = jnp.dot(grad_gate, gate_cols.T, preferred_element_type=jnp.float32)
    row_grad = row_grad + jnp.dot(grad_up, up_cols.T, preferred_element_type=jnp.float32)
    return row_grad, scores


def reference(tokens_in, d_out, gates, expert_ids, slot_ids, w_gate, w_up, w_down):
    block_rows = TOKENS // TOK_DEV * CAP
    token_index = jnp.arange(TOKENS, dtype=jnp.int32)
    position = ((token_index // TOK_DEV)[:, None] * CAP + slot_ids).astype(jnp.int32)
    flat_expert = expert_ids.reshape(-1).astype(jnp.int32)
    flat_place = position.reshape(-1)
    flat_token = jnp.repeat(token_index, 2)
    token_lookup = jnp.zeros((EXPERTS, block_rows), jnp.int32).at[flat_expert, flat_place].set(flat_token)
    filled = jnp.zeros((EXPERTS, block_rows), jnp.int32).at[flat_expert, flat_place].set(1)

    def one_expert(expert):
        chosen = token_lookup[expert]
        keep_row = filled[expert][:, None] == 1
        rows_in = jnp.where(keep_row, tokens_in[chosen], jnp.zeros((), tokens_in.dtype))
        rows_back = jnp.where(keep_row, d_out[chosen], jnp.zeros((), d_out.dtype))
        return expert_pass(expert, rows_in, rows_back, w_gate, w_up, w_down)

    row_grads, scores = lax.map(one_expert, jnp.arange(EXPERTS, dtype=jnp.int32))
    per_row = row_grads[flat_expert, flat_place].reshape(TOKENS, 2, D)
    d_tokens = jnp.sum(per_row * gates[:, :, None], axis=1).astype(jnp.bfloat16)
    d_gates = scores[flat_expert, flat_place].reshape(TOKENS, 2)
    return d_tokens, d_gates
```

```python
import jax
import jax.numpy as jnp
from jax import lax
from jax.experimental import pallas as pl
from jax.experimental.pallas import tpu as pltpu
from jax.sharding import PartitionSpec as P

MESH = pl.DeviceIdType.MESH
HIGH = lax.Precision.HIGHEST
EXPERTS = 8
CAP = 6
TOK = 16
NZ = 8
FEAT = 384
HID = 256
BLK = 48
HALF = 192
ROWS = 384
SUB = HALF // 2


def iota(shape, dim):
    return lax.broadcasted_iota(jnp.int32, shape, dim)


def div6(v):
    return (v * 43) >> 8


def kernel(
    tok, dout, gates, ids, slots, wg, wu, wd, d_tok, d_gate,
    wgu, wdn, send, drecv, G, acc_gu, acc_b, gcat, part, pair, rsend, rrecv, lsend, lrecv,
    total, ysend, yrecv, ret, rrecv2, scz, scy, scc, scs,
    w_sem, d_ss, d_rs, y_ss, y_rs, r_ss, r_rs, l_ss, l_rs, f_ss, f_rs,
    p_ss, p_rs, rr_ss, rr_rs, rl_ss, rl_rs, yy_ss, yy_rs, t_ss, t_rs, z_ss, z_rs, s_ss, s_rs, c_ss, c_rs,
):
    ep = lax.axis_index("ep")
    z = lax.axis_index("tp")
    own = lax.div(ep, 8)
    place = lax.rem(ep, 8)
    yl = lax.div(place, 2)
    c = lax.rem(place, 2)
    other = 1 - c

    def at_expert(e):
        return (e * 8 + place, z)

    def at_y(yy):
        return (own * 8 + yy * 2 + c, z)

    def at_z(zz):
        return (ep, zz)

    sibling = (own * 8 + yl * 2 + other, z)

    def copy(src, dst, ss, rs, dev):
        return pltpu.make_async_remote_copy(
            src_ref=src, dst_ref=dst, send_sem=ss, recv_sem=rs, device_id=dev, device_id_type=MESH
        )

    loads = [
        pltpu.make_async_copy(wg, wgu.at[:, pl.ds(0, HID)], w_sem.at[0]),
        pltpu.make_async_copy(wu, wgu.at[:, pl.ds(HID, HID)], w_sem.at[1]),
        pltpu.make_async_copy(wd, wdn, w_sem.at[2]),
    ]
    for ld in loads:
        ld.start()

    barrier = pltpu.get_barrier_semaphore()
    peers = [at_expert(lax.rem(own + i, 8)) for i in range(1, 8)]
    peers += [at_y(lax.rem(yl + i, 4)) for i in range(1, 4)]
    peers += [at_z(lax.rem(z + i, NZ)) for i in range(1, NZ)]
    peers += [sibling]
    for dev in peers:
        pl.semaphore_signal(barrier, inc=1, device_id=dev, device_id_type=MESH)

    r = iota((128, TOK), 0)
    pick = jnp.zeros((128, TOK), jnp.float32)
    for k in range(2):
        hit = (ids[k : k + 1, :] == (r >> 4)) & (slots[k : k + 1, :] == (r & 7))
        pick = pick + hit.astype(jnp.float32)
    is_back = (r & 8) == 8
    pick_in = jnp.where(is_back, 0.0, pick).astype(jnp.bfloat16)
    pick_back = jnp.where(is_back, pick, 0.0).astype(jnp.bfloat16)
    placed = jnp.dot(pick_in, tok[...], preferred_element_type=jnp.float32)
    placed = placed + jnp.dot(pick_back, dout[...], preferred_element_type=jnp.float32)
    send[...] = placed.astype(jnp.bfloat16).reshape(EXPERTS, 16, FEAT)

    pl.semaphore_wait(barrier, len(peers))

    waits = []
    disp = []
    for i in range(1, 8):
        e = lax.rem(own + i, 8)
        cp = copy(send.at[e], drecv.at[own], d_ss.at[i], d_rs.at[i], at_expert(e))
        cp.start()
        disp.append(cp)
    drecv[own] = send[own]
    for i in range(1, 8):
        j = lax.rem(own + 8 - i, 8)
        copy(send.at[j], drecv.at[j], d_ss.at[i], d_rs.at[i], at_expert(j)).wait_recv()
    waits += disp

    r = iota((2 * BLK, 128), 0)
    back = (r >= BLK).astype(jnp.int32)
    q = r - back * BLK
    j6 = div6(q)
    sel = (iota((2 * BLK, 128), 1) == j6 * 16 + back * 8 + (q - 6 * j6)).astype(jnp.bfloat16)
    dense = jnp.dot(sel, drecv[...].reshape(128, FEAT), preferred_element_type=jnp.float32)
    dense = dense.astype(jnp.bfloat16)
    G[z, 0, c, yl] = dense[:BLK]
    G[z, 1, c, yl] = dense[BLK:]

    for i in range(1, 4):
        yy = lax.rem(yl + i, 4)
        blk = G.at[z, :, c, yl]
        cp = copy(blk, blk, y_ss.at[i], y_rs.at[i], at_y(yy))
        cp.start()
        waits.append(cp)
    for i in range(1, 4):
        yy = lax.rem(yl + 4 - i, 4)
        blk = G.at[z, :, c, yy]
        copy(blk, blk, y_ss.at[i], y_rs.at[i], at_y(yy)).wait_recv()

    acc_gu[...] = jnp.zeros_like(acc_gu)
    acc_b[...] = jnp.zeros_like(acc_b)

    def right(k, a):
        blk = G.at[lax.rem(z + NZ - k, NZ), a, c]
        return copy(blk, blk, r_ss.at[k, a], r_rs.at[k, a], at_z(lax.rem(z + 1, NZ)))

    def right_got(k, a):
        blk = G.at[lax.rem(z + NZ - 1 - k, NZ), a, c]
        return copy(blk, blk, r_ss.at[k, a], r_rs.at[k, a], at_z(lax.rem(z + 1, NZ)))

    def left(k, a):
        blk = G.at[lax.rem(z + k, NZ), a, c]
        return copy(blk, blk, l_ss.at[k, a], l_rs.at[k, a], at_z(lax.rem(z + NZ - 1, NZ)))

    def left_got(k, a):
        blk = G.at[lax.rem(z + k + 1, NZ), a, c]
        return copy(blk, blk, l_ss.at[k, a], l_rs.at[k, a], at_z(lax.rem(z + NZ - 1, NZ)))

    def forward(slot, a, n):
        blk = G.at[slot, a, c]
        return copy(blk, blk, f_ss.at[n, a], f_rs.at[n, a], sibling)

    def forwarded(slot, a, n):
        blk = G.at[slot, a, other]
        return copy(blk, blk, f_ss.at[n, a], f_rs.at[n, a], sibling)

    def slot_of(n):
        if n == 0:
            return z
        if n <= 3:
            return lax.rem(z + NZ - n, NZ)
        if n <= 6:
            return lax.rem(z + n - 3, NZ)
        return lax.rem(z + 4, NZ)

    def products(slot):
        base = pl.multiple_of(slot * FEAT, FEAT)
        rows_in = G[slot, 0].reshape(ROWS, FEAT)
        rows_back = G[slot, 1].reshape(ROWS, FEAT)
        acc_gu[...] += jnp.dot(
            rows_in, wgu[pl.ds(base, FEAT), :], preferred_element_type=jnp.float32
        )
        acc_b[...] += lax.dot_general(
            rows_back, wdn[:, pl.ds(base, FEAT)], (((1,), (1,)), ((), ())),
            preferred_element_type=jnp.float32,
        )

    def start(cp):
        cp.start()
        waits.append(cp)

    for a in range(2):
        start(right(0, a))
        start(left(0, a))
        start(forward(z, a, 0))
    for ld in loads:
        ld.wait()
    for k in range(4):
        ready = [0] if k == 0 else [k, k + 3]
        if k < 3:
            for a in range(2):
                right_got(k, a).wait_recv()
                if k < 2 or a == 0:
                    start(right(k + 1, a))
                start(forward(slot_of(k + 1), a, k + 1))
                left_got(k, a).wait_recv()
                if k < 2 or a == 1:
                    start(left(k + 1, a))
                start(forward(slot_of(k + 4), a, k + 4))
        else:
            right_got(3, 0).wait_recv()
            start(forward(slot_of(7), 0, 7))
            left_got(3, 1).wait_recv()
            start(forward(slot_of(7), 1, 7))
            ready = ready + [7]
        for n in ready:
            for a in range(2):
                forwarded(slot_of(n), a, n).wait_recv()
            products(slot_of(n))

    gate = acc_gu[:, :HID]
    up = acc_gu[:, HID:]
    bg = acc_b[...]
    sg = jax.nn.sigmoid(gate)
    silu = gate * sg
    gcat[:, :HID] = (bg * up * sg * (1.0 + gate * (1.0 - sg))).astype(jnp.bfloat16)
    gcat[:, HID:] = (bg * silu).astype(jnp.bfloat16)
    score = jnp.sum(silu * up * bg, axis=1, keepdims=True)

    q = iota((ROWS, 128), 0)
    for v in (4, 2, 1):
        q = jnp.where(q >= v * BLK, q - v * BLK, q)
    j6 = div6(q)
    spread = jnp.where(iota((ROWS, 128), 1) == j6 * 8 + (q - 6 * j6), score, 0.0)
    g = iota((8, ROWS), 0)
    n = iota((8, ROWS), 1)
    mine = ((n >= g * BLK) & (n < g * BLK + BLK)).astype(jnp.float32)
    scz[z] = jnp.dot(mine, spread, precision=HIGH, preferred_element_type=jnp.float32)
    for i in range(1, NZ):
        zz = lax.rem(z + i, NZ)
        start(copy(scz.at[z], scz.at[z], z_ss.at[i], z_rs.at[i], at_z(zz)))

    def slice_grad(slot):
        base = pl.multiple_of(slot * FEAT, FEAT)
        part[slot] = lax.dot_general(
            gcat[...], wgu[pl.ds(base, FEAT), :], (((1,), (1,)), ((), ())),
            preferred_element_type=jnp.float32,
        ).reshape(2, HALF, FEAT)

    def pair_send(slot, n):
        return copy(part.at[slot, other], pair.at[slot], p_ss.at[n], p_rs.at[n], sibling)

    order = [7, 3, 6, 2, 5, 1, 4, 0]
    for n in order:
        slice_grad(slot_of(n))
        start(pair_send(slot_of(n), n))

    def pair_sum(n, lo, size):
        slot = slot_of(n)
        return part[slot, c, lo : lo + size, :] + pair[slot, lo : lo + size, :]

    def pair_wait(n):
        pair_send(slot_of(n), n).wait_recv()

    def ring_r(k):
        rows = pl.ds(0, SUB) if k == 0 else pl.ds(0, HALF)
        return copy(
            rsend.at[k, rows], rrecv.at[k, rows], rr_ss.at[k], rr_rs.at[k],
            at_z(lax.rem(z + 1, NZ)),
        )

    def ring_l(k):
        rows = pl.ds(SUB, SUB) if k == 0 else pl.ds(0, HALF)
        return copy(
            lsend.at[k, rows], lrecv.at[k, rows], rl_ss.at[k], rl_rs.at[k],
            at_z(lax.rem(z + NZ - 1, NZ)),
        )

    pair_wait(7)
    rsend[0, :SUB] = pair_sum(7, 0, SUB).astype(jnp.bfloat16)
    start(ring_r(0))
    lsend[0, SUB:] = pair_sum(7, SUB, SUB).astype(jnp.bfloat16)
    start(ring_l(0))
    for k in range(1, 4):
        nr, nl = 7 - k, 4 - k
        pair_wait(nr)
        pair_wait(nl)
        if k == 1:
            rsend[1, SUB:] = pair_sum(nr, SUB, SUB).astype(jnp.bfloat16)
            lsend[1, :SUB] = pair_sum(nl, 0, SUB).astype(jnp.bfloat16)
            ring_r(0).wait_recv()
            rsend[1, :SUB] = (pair_sum(nr, 0, SUB) + rrecv[0, :SUB].astype(jnp.float32)).astype(
                jnp.bfloat16
            )
            start(ring_r(1))
            ring_l(0).wait_recv()
            lsend[1, SUB:] = (
                pair_sum(nl, SUB, SUB) + lrecv[0, SUB:].astype(jnp.float32)
            ).astype(jnp.bfloat16)
            start(ring_l(1))
        else:
            ring_r(k - 1).wait_recv()
            rsend[k] = (pair_sum(nr, 0, HALF) + rrecv[k - 1].astype(jnp.float32)).astype(
                jnp.bfloat16
            )
            start(ring_r(k))
            ring_l(k - 1).wait_recv()
            lsend[k] = (pair_sum(nl, 0, HALF) + lrecv[k - 1].astype(jnp.float32)).astype(
                jnp.bfloat16
            )
            start(ring_l(k))
        if k == 2:
            for i in range(1, NZ):
                zz = lax.rem(z + NZ - i, NZ)
                copy(scz.at[zz], scz.at[zz], z_ss.at[i], z_rs.at[i], at_z(zz)).wait_recv()
            scy[yl] = jnp.sum(scz[...], axis=0)
            for i in range(1, 4):
                yy = lax.rem(yl + i, 4)
                start(copy(scy.at[yl], scy.at[yl], s_ss.at[i], s_rs.at[i], at_y(yy)))
        if k == 3:
            for i in range(1, 4):
                yy = lax.rem(yl + 4 - i, 4)
                copy(scy.at[yy], scy.at[yy], s_ss.at[i], s_rs.at[i], at_y(yy)).wait_recv()
            scc[c] = jnp.sum(scy[...], axis=0)
            start(copy(scc.at[c], scc.at[c], c_ss, c_rs, sibling))
    pair_wait(0)
    copy(scc.at[other], scc.at[other], c_ss, c_rs, sibling).wait_recv()
    scs[...] = scc[0] + scc[1]
    ring_r(3).wait_recv()
    ring_l(3).wait_recv()
    summed = pair_sum(0, 0, HALF) + rrecv[3].astype(jnp.float32) + lrecv[3].astype(jnp.float32)
    total[...] = summed.reshape(4, BLK, FEAT)
    ysend[...] = summed.astype(jnp.bfloat16).reshape(4, BLK, FEAT)
    for i in range(1, 4):
        yy = lax.rem(yl + i, 4)
        start(copy(ysend.at[yy], yrecv.at[i], yy_ss.at[i], yy_rs.at[i], at_y(yy)))
    rows = total[yl]
    for i in range(1, 4):
        copy(ysend.at[0], yrecv.at[i], yy_ss.at[i], yy_rs.at[i], at_y(yl)).wait_recv()
        rows = rows + yrecv[i].astype(jnp.float32)

    r = iota((64, BLK), 0)
    pos = iota((64, BLK), 1)
    sel = (((r & 7) < CAP) & (pos == (r >> 3) * 6 + (r & 7))).astype(jnp.float32)
    ret[:, :, :FEAT] = jnp.dot(
        sel, rows, precision=HIGH, preferred_element_type=jnp.float32
    ).reshape(EXPERTS, 8, FEAT)
    ret[:, :, FEAT:] = jnp.broadcast_to(scs[...][None], (EXPERTS, 8, 128))
    for i in range(1, 8):
        e = lax.rem(own + i, 8)
        start(copy(ret.at[e], rrecv2.at[own], t_ss.at[i], t_rs.at[i], at_expert(e)))
    rrecv2[own] = ret[own]
    r = iota((64, TOK), 0)
    hits = []
    weight = jnp.zeros((64, TOK), jnp.float32)
    for k in range(2):
        hit = (ids[k : k + 1, :] == (r >> 3)) & (slots[k : k + 1, :] == (r & 7))
        hits.append(hit)
        weight = weight + jnp.where(hit, gates[k : k + 1, :], 0.0)
    for i in range(1, 8):
        j = lax.rem(own + 8 - i, 8)
        copy(ret.at[j], rrecv2.at[j], t_ss.at[i], t_rs.at[i], at_expert(j)).wait_recv()
    d_tok[...] = lax.dot_general(
        weight, rrecv2[:, :, :FEAT].reshape(64, FEAT), (((0,), (0,)), ((), ())),
        precision=HIGH, preferred_element_type=jnp.float32,
    ).astype(jnp.bfloat16)
    sc = rrecv2[:, :, FEAT:]
    row = c * 4 + yl
    sc = jnp.sum(jnp.where(iota((EXPERTS, 8, 128), 1) == row, sc, 0.0), axis=1, keepdims=True)
    sc = jnp.broadcast_to(sc, (EXPERTS, 8, 128)).reshape(64, 128)
    lane = own * 8 + (iota((64, 128), 0) & 7)
    sc = jnp.sum(jnp.where(iota((64, 128), 1) == lane, sc, 0.0), axis=1, keepdims=True)
    for k in range(2):
        d_gate[k : k + 1, :] = jnp.sum(jnp.where(hits[k], sc, 0.0), axis=0, keepdims=True)
    for cp in waits:
        cp.wait_send()


def local(tokens_in, d_out, gates, expert_ids, slot_ids, w_gate, w_up, w_down):
    vmem = pl.BlockSpec(memory_space=pltpu.VMEM)
    hbm = pl.BlockSpec(memory_space=pl.ANY)
    bf, f32, dma = jnp.bfloat16, jnp.float32, pltpu.SemaphoreType.DMA
    scratch = [
        pltpu.VMEM((NZ * FEAT, 2 * HID), bf),
        pltpu.VMEM((HID, NZ * FEAT), bf),
        pltpu.VMEM((EXPERTS, 16, FEAT), bf),
        pltpu.VMEM((EXPERTS, 16, FEAT), bf),
        pltpu.VMEM((NZ, 2, 2, 4, BLK, FEAT), bf),
        pltpu.VMEM((ROWS, 2 * HID), f32),
        pltpu.VMEM((ROWS, HID), f32),
        pltpu.VMEM((ROWS, 2 * HID), bf),
        pltpu.VMEM((NZ, 2, HALF, FEAT), f32),
        pltpu.VMEM((NZ, HALF, FEAT), f32),
        pltpu.VMEM((4, HALF, FEAT), bf),
        pltpu.VMEM((4, HALF, FEAT), bf),
        pltpu.VMEM((4, HALF, FEAT), bf),
        pltpu.VMEM((4, HALF, FEAT), bf),
        pltpu.VMEM((4, BLK, FEAT), f32),
        pltpu.VMEM((4, BLK, FEAT), bf),
        pltpu.VMEM((4, BLK, FEAT), bf),
        pltpu.VMEM((EXPERTS, 8, FEAT + 128), f32),
        pltpu.VMEM((EXPERTS, 8, FEAT + 128), f32),
        pltpu.VMEM((NZ, 8, 128), f32),
        pltpu.VMEM((4, 8, 128), f32),
        pltpu.VMEM((2, 8, 128), f32),
        pltpu.VMEM((8, 128), f32),
        dma((3,)),
        dma((8,)), dma((8,)),
        dma((4,)), dma((4,)),
        dma((4, 2)), dma((4, 2)),
        dma((4, 2)), dma((4, 2)),
        dma((8, 2)), dma((8, 2)),
        dma((8,)), dma((8,)),
        dma((4,)), dma((4,)),
        dma((4,)), dma((4,)),
        dma((4,)), dma((4,)),
        dma((8,)), dma((8,)),
        dma((8,)), dma((8,)),
        dma((4,)), dma((4,)),
        dma, dma,
    ]
    d_tok, d_gate = pl.pallas_call(
        kernel,
        out_shape=(
            jax.ShapeDtypeStruct((TOK, FEAT), bf),
            jax.ShapeDtypeStruct((2, TOK), f32),
        ),
        in_specs=[vmem] * 5 + [hbm] * 3,
        out_specs=(vmem, vmem),
        scratch_shapes=scratch,
        name="moe_dx",
        compiler_params=pltpu.CompilerParams(
            collective_id=0, has_side_effects=True, vmem_limit_bytes=48 * 2**20
        ),
        cost_estimate=pl.CostEstimate(
            flops=5 * 2 * ROWS * NZ * FEAT * HID, bytes_accessed=6 * NZ * FEAT * HID, transcendentals=ROWS * HID
        ),
    )(tokens_in, d_out, gates.T, expert_ids.T, slot_ids.T, w_gate, w_up, w_down)
    return d_tok, d_gate.T


def solution(mesh):
    placed = (
        P("ep", "tp"),
        P("ep", "tp"),
        P("ep", None),
        P("ep", None),
        P("ep", None),
        P(None, ("ep", "tp")),
        P(None, ("ep", "tp")),
        P(("ep", "tp"), None),
    )
    return jax.shard_map(
        local, mesh=mesh, in_specs=placed, out_specs=(P("ep", "tp"), P("ep", None)), check_vma=False
    )
```

```python
import jax
import jax.numpy as jnp
from jax import lax
from jax.experimental import pallas as pl
from jax.experimental.pallas import tpu as pltpu
from jax.sharding import PartitionSpec as P

MESH = pl.DeviceIdType.MESH
HIGH = lax.Precision.HIGHEST
EXPERTS = 8
CAP = 6
TOK = 16
NZ = 8
FEAT = 384
HID = 256
BLK = 48
HALF = 192
SUB = HALF // 2


def iota(shape, dim):
    return lax.broadcasted_iota(jnp.int32, shape, dim)


def div6(v):
    return (v * 43) >> 8


def kernel(
    tok_h, dout_h, gates_h, ids_h, slots_h, wg, wu, wd, d_tok, d_gate,
    tok, dout, gates, ids, slots, wgu, wdn, send, drecv, G, acc_gu, acc_b, gcat, part,
    rsend, rrecv, lsend, lrecv, total, ysend, yrecv, ret, back, scz, scy, scs,
    i_sem, w_sem, p_ss, p_rs, d_ss, d_rs, y_ss, y_rs, r_ss, r_rs, l_ss, l_rs,
    rr_ss, rr_rs, rl_ss, rl_rs, yy_ss, yy_rs, t_ss, t_rs, z_ss, z_rs, s_ss, s_rs,
):
    ep = lax.axis_index("ep")
    z = lax.axis_index("tp")
    own = lax.div(ep, 8)
    place = lax.rem(ep, 8)
    yl = lax.div(place, 2)
    c = lax.rem(place, 2)

    def at_expert(e):
        mirrored = lax.rem(own + e, 2)
        return (e * 8 + (yl + mirrored * (3 - 2 * yl)) * 2 + c, z)

    def at_y(yy):
        return (own * 8 + yy * 2 + c, z)

    def at_z(zz):
        return (ep, zz)

    sibling = (own * 8 + yl * 2 + 1 - c, z)

    def copy(src, dst, ss, rs, dev):
        return pltpu.make_async_remote_copy(
            src_ref=src, dst_ref=dst, send_sem=ss, recv_sem=rs, device_id=dev, device_id_type=MESH
        )

    waits = []

    def start(cp):
        cp.start()
        waits.append(cp)

    def weights(core):
        at = pl.multiple_of(core * HID, HID)
        return (
            (wg, wgu.at[:, pl.ds(at, HID)]),
            (wu, wgu.at[:, pl.ds(pl.multiple_of(at + 2 * HID, HID), HID)]),
            (wd, wdn.at[pl.ds(at, HID), :]),
        )

    small = [
        pltpu.make_async_copy(src, dst, i_sem.at[i])
        for i, (src, dst) in enumerate(
            ((ids_h, ids), (slots_h, slots), (tok_h, tok), (dout_h, dout), (gates_h, gates))
        )
    ]
    loads = [
        pltpu.make_async_copy(src, dst, w_sem.at[i]) for i, (src, dst) in enumerate(weights(c))
    ]
    for ld in small + loads:
        ld.start()

    barrier = pltpu.get_barrier_semaphore()
    peers = [at_expert(lax.rem(own + i, 8)) for i in range(1, 8)]
    peers += [at_y(lax.rem(yl + i, 4)) for i in range(1, 4)]
    peers += [at_z(lax.rem(z + i, NZ)) for i in range(1, NZ)]
    peers += [sibling]
    for dev in peers:
        pl.semaphore_signal(barrier, inc=1, device_id=dev, device_id_type=MESH)

    for ld in small:
        ld.wait()
    r = iota((128, TOK), 0)
    pick = jnp.zeros((128, TOK), jnp.float32)
    for k in range(2):
        hit = (ids[k : k + 1, :] == (r >> 4)) & (slots[k : k + 1, :] == (r & 7))
        pick = pick + hit.astype(jnp.float32)
    is_back = (r & 8) == 8
    pick_in = jnp.where(is_back, 0.0, pick).astype(jnp.bfloat16)
    pick_back = jnp.where(is_back, pick, 0.0).astype(jnp.bfloat16)
    placed = jnp.dot(pick_in, tok[...], preferred_element_type=jnp.float32)
    placed = placed + jnp.dot(pick_back, dout[...], preferred_element_type=jnp.float32)
    send[...] = placed.astype(jnp.bfloat16).reshape(EXPERTS, 16, FEAT)

    pl.semaphore_wait(barrier, len(peers))

    for i in range(1, 8):
        e = lax.rem(own + i, 8)
        start(copy(send.at[e], drecv.at[own], d_ss.at[i], d_rs.at[i], at_expert(e)))
    for i, (src, dst) in enumerate(weights(c)):
        start(copy(src, dst, p_ss.at[i], p_rs.at[i], sibling))
    drecv[own] = send[own]
    r = iota((2 * BLK, 128), 0)
    second = (r >= BLK).astype(jnp.int32)
    q = r - second * BLK
    j6 = div6(q)
    sel = (iota((2 * BLK, 128), 1) == j6 * 16 + second * 8 + (q - 6 * j6)).astype(jnp.bfloat16)
    for i in range(1, 8):
        j = lax.rem(own + 8 - i, 8)
        copy(send.at[j], drecv.at[j], d_ss.at[i], d_rs.at[i], at_expert(j)).wait_recv()
    dense = jnp.dot(sel, drecv[...].reshape(128, FEAT), preferred_element_type=jnp.float32)
    dense = dense.astype(jnp.bfloat16)
    G[z, 0, yl] = dense[:BLK]
    G[z, 1, yl] = dense[BLK:]

    for i in range(1, 4):
        yy = lax.rem(yl + i, 4)
        blk = G.at[z, :, yl]
        start(copy(blk, blk, y_ss.at[i], y_rs.at[i], at_y(yy)))
    acc_gu[...] = jnp.zeros_like(acc_gu)
    acc_b[...] = jnp.zeros_like(acc_b)
    for i in range(1, 4):
        yy = lax.rem(yl + 4 - i, 4)
        blk = G.at[z, :, yy]
        copy(blk, blk, y_ss.at[i], y_rs.at[i], at_y(yy)).wait_recv()

    def right(k, a):
        blk = G.at[lax.rem(z + NZ - k, NZ), a]
        return copy(blk, blk, r_ss.at[k, a], r_rs.at[k, a], at_z(lax.rem(z + 1, NZ)))

    def right_got(k, a):
        blk = G.at[lax.rem(z + NZ - 1 - k, NZ), a]
        return copy(blk, blk, r_ss.at[k, a], r_rs.at[k, a], at_z(lax.rem(z + 1, NZ)))

    def left(k, a):
        blk = G.at[lax.rem(z + k, NZ), a]
        return copy(blk, blk, l_ss.at[k, a], l_rs.at[k, a], at_z(lax.rem(z + NZ - 1, NZ)))

    def left_got(k, a):
        blk = G.at[lax.rem(z + k + 1, NZ), a]
        return copy(blk, blk, l_ss.at[k, a], l_rs.at[k, a], at_z(lax.rem(z + NZ - 1, NZ)))

    def slot_of(n):
        if n == 0:
            return z
        if n <= 3:
            return lax.rem(z + NZ - n, NZ)
        if n <= 6:
            return lax.rem(z + n - 3, NZ)
        return lax.rem(z + 4, NZ)

    def products(slot):
        base = pl.multiple_of(slot * FEAT, FEAT)
        rows_in = G[slot, 0].reshape(HALF, FEAT)
        rows_back = G[slot, 1].reshape(HALF, FEAT)
        acc_gu[...] += jnp.dot(
            rows_in, wgu[pl.ds(base, FEAT), :], preferred_element_type=jnp.float32
        )
        acc_b[...] += lax.dot_general(
            rows_back, wdn[:, pl.ds(base, FEAT)], (((1,), (1,)), ((), ())),
            preferred_element_type=jnp.float32,
        )

    for a in range(2):
        start(right(0, a))
        start(left(0, a))
    for ld in loads:
        ld.wait()
    for i, (src, dst) in enumerate(weights(1 - c)):
        copy(src, dst, p_ss.at[i], p_rs.at[i], sibling).wait_recv()
    products(z)
    for k in range(3):
        for a in range(2):
            right_got(k, a).wait_recv()
            if k < 2 or a == 0:
                start(right(k + 1, a))
            left_got(k, a).wait_recv()
            if k < 2 or a == 1:
                start(left(k + 1, a))
        products(slot_of(k + 1))
        products(slot_of(k + 4))
    right_got(3, 0).wait_recv()
    left_got(3, 1).wait_recv()
    products(slot_of(7))

    gate = acc_gu[:, : 2 * HID]
    up = acc_gu[:, 2 * HID :]
    bg = acc_b[...]
    sg = jax.nn.sigmoid(gate)
    silu = gate * sg
    gcat[:, : 2 * HID] = (bg * up * sg * (1.0 + gate * (1.0 - sg))).astype(jnp.bfloat16)
    gcat[:, 2 * HID :] = (bg * silu).astype(jnp.bfloat16)
    score = jnp.sum(silu * up * bg, axis=1, keepdims=True)

    def slice_grad(slot):
        base = pl.multiple_of(slot * FEAT, FEAT)
        part[slot] = lax.dot_general(
            gcat[...], wgu[pl.ds(base, FEAT), :], (((1,), (1,)), ((), ())),
            preferred_element_type=jnp.float32,
        )

    def ring_r(k):
        rows = pl.ds(0, SUB) if k == 0 else pl.ds(0, HALF)
        return copy(
            rsend.at[k, rows], rrecv.at[k, rows], rr_ss.at[k], rr_rs.at[k],
            at_z(lax.rem(z + 1, NZ)),
        )

    def ring_l(k):
        rows = pl.ds(SUB, SUB) if k == 0 else pl.ds(0, HALF)
        return copy(
            lsend.at[k, rows], lrecv.at[k, rows], rl_ss.at[k], rl_rs.at[k],
            at_z(lax.rem(z + NZ - 1, NZ)),
        )

    slice_grad(slot_of(7))
    rsend[0, :SUB] = part[slot_of(7), :SUB].astype(jnp.bfloat16)
    start(ring_r(0))
    lsend[0, SUB:] = part[slot_of(7), SUB:].astype(jnp.bfloat16)
    start(ring_l(0))

    q = iota((HALF, 128), 0)
    for v in (2, 1):
        q = jnp.where(q >= v * BLK, q - v * BLK, q)
    j6 = div6(q)
    spread = jnp.where(iota((HALF, 128), 1) == j6 * 8 + (q - 6 * j6), score, 0.0)
    g = iota((8, HALF), 0)
    n = iota((8, HALF), 1)
    mine = ((n >= g * BLK) & (n < g * BLK + BLK)).astype(jnp.float32)
    scz[z] = jnp.dot(mine, spread, precision=HIGH, preferred_element_type=jnp.float32)
    for i in range(1, NZ):
        start(copy(scz.at[z], scz.at[z], z_ss.at[i], z_rs.at[i], at_z(lax.rem(z + i, NZ))))

    for k in range(1, 4):
        nr, nl = slot_of(7 - k), slot_of(4 - k)
        slice_grad(nr)
        slice_grad(nl)
        ring_r(k - 1).wait_recv()
        if k == 1:
            rsend[1, SUB:] = part[nr, SUB:].astype(jnp.bfloat16)
            rsend[1, :SUB] = (part[nr, :SUB] + rrecv[0, :SUB].astype(jnp.float32)).astype(
                jnp.bfloat16
            )
        else:
            rsend[k] = (part[nr] + rrecv[k - 1].astype(jnp.float32)).astype(jnp.bfloat16)
        start(ring_r(k))
        ring_l(k - 1).wait_recv()
        if k == 1:
            lsend[1, :SUB] = part[nl, :SUB].astype(jnp.bfloat16)
            lsend[1, SUB:] = (part[nl, SUB:] + lrecv[0, SUB:].astype(jnp.float32)).astype(
                jnp.bfloat16
            )
        else:
            lsend[k] = (part[nl] + lrecv[k - 1].astype(jnp.float32)).astype(jnp.bfloat16)
        start(ring_l(k))
        if k == 2:
            for i in range(1, NZ):
                zz = lax.rem(z + NZ - i, NZ)
                copy(scz.at[zz], scz.at[zz], z_ss.at[i], z_rs.at[i], at_z(zz)).wait_recv()
            scy[yl] = jnp.sum(scz[...], axis=0)
            for i in range(1, 4):
                yy = lax.rem(yl + i, 4)
                start(copy(scy.at[yl], scy.at[yl], s_ss.at[i], s_rs.at[i], at_y(yy)))
    slice_grad(z)
    for i in range(1, 4):
        yy = lax.rem(yl + 4 - i, 4)
        copy(scy.at[yy], scy.at[yy], s_ss.at[i], s_rs.at[i], at_y(yy)).wait_recv()
    scs[...] = jnp.sum(scy[...], axis=0)
    ring_r(3).wait_recv()
    ring_l(3).wait_recv()
    summed = part[z] + rrecv[3].astype(jnp.float32) + lrecv[3].astype(jnp.float32)
    total[...] = summed.reshape(4, BLK, FEAT)
    ysend[...] = summed.astype(jnp.bfloat16).reshape(4, BLK, FEAT)
    for i in range(1, 4):
        yy = lax.rem(yl + i, 4)
        start(copy(ysend.at[yy], yrecv.at[i], yy_ss.at[i], yy_rs.at[i], at_y(yy)))
    rows = total[yl]
    for i in range(1, 4):
        copy(ysend.at[0], yrecv.at[i], yy_ss.at[i], yy_rs.at[i], at_y(yl)).wait_recv()
        rows = rows + yrecv[i].astype(jnp.float32)

    r = iota((64, BLK), 0)
    pos = iota((64, BLK), 1)
    sel = (((r & 7) < CAP) & (pos == (r >> 3) * 6 + (r & 7))).astype(jnp.float32)
    ret[:, :, :FEAT] = jnp.dot(
        sel, rows, precision=HIGH, preferred_element_type=jnp.float32
    ).reshape(EXPERTS, 8, FEAT)
    ret[:, :, FEAT:] = jnp.broadcast_to(scs[...][None], (EXPERTS, 8, 128))
    for i in range(1, 8):
        e = lax.rem(own + i, 8)
        start(copy(ret.at[e], back.at[own], t_ss.at[i], t_rs.at[i], at_expert(e)))
    back[own] = ret[own]
    r = iota((64, TOK), 0)
    hits = []
    weight = jnp.zeros((64, TOK), jnp.float32)
    for k in range(2):
        hit = (ids[k : k + 1, :] == (r >> 3)) & (slots[k : k + 1, :] == (r & 7))
        hits.append(hit)
        weight = weight + jnp.where(hit, gates[k : k + 1, :], 0.0)
    for i in range(1, 8):
        j = lax.rem(own + 8 - i, 8)
        copy(ret.at[j], back.at[j], t_ss.at[i], t_rs.at[i], at_expert(j)).wait_recv()
    d_tok[...] = lax.dot_general(
        weight, back[:, :, :FEAT].reshape(64, FEAT), (((0,), (0,)), ((), ())),
        precision=HIGH, preferred_element_type=jnp.float32,
    ).astype(jnp.bfloat16)
    sc = back[:, :, FEAT:]
    same = lax.rem(iota((EXPERTS, 8, 128), 0) + own, 2) == 0
    row = jnp.where(same, yl, 3 - yl)
    sc = jnp.sum(jnp.where(iota((EXPERTS, 8, 128), 1) == row, sc, 0.0), axis=1, keepdims=True)
    sc = jnp.broadcast_to(sc, (EXPERTS, 8, 128)).reshape(64, 128)
    lane = own * 8 + (iota((64, 128), 0) & 7)
    sc = jnp.sum(jnp.where(iota((64, 128), 1) == lane, sc, 0.0), axis=1, keepdims=True)
    for k in range(2):
        d_gate[k : k + 1, :] = jnp.sum(jnp.where(hits[k], sc, 0.0), axis=0, keepdims=True)
    for cp in waits:
        cp.wait_send()


def local(tokens_in, d_out, gates, expert_ids, slot_ids, w_gate, w_up, w_down):
    vmem = pl.BlockSpec(memory_space=pltpu.VMEM)
    hbm = pl.BlockSpec(memory_space=pltpu.HBM)
    bf, f32, dma = jnp.bfloat16, jnp.float32, pltpu.SemaphoreType.DMA
    scratch = [
        pltpu.VMEM((TOK, FEAT), bf),
        pltpu.VMEM((TOK, FEAT), bf),
        pltpu.VMEM((2, TOK), f32),
        pltpu.VMEM((2, TOK), jnp.int32),
        pltpu.VMEM((2, TOK), jnp.int32),
        pltpu.VMEM((NZ * FEAT, 4 * HID), bf),
        pltpu.VMEM((2 * HID, NZ * FEAT), bf),
        pltpu.VMEM((EXPERTS, 16, FEAT), bf),
        pltpu.VMEM((EXPERTS, 16, FEAT), bf),
        pltpu.VMEM((NZ, 2, 4, BLK, FEAT), bf),
        pltpu.VMEM((HALF, 4 * HID), f32),
        pltpu.VMEM((HALF, 2 * HID), f32),
        pltpu.VMEM((HALF, 4 * HID), bf),
        pltpu.VMEM((NZ, HALF, FEAT), f32),
        pltpu.VMEM((4, HALF, FEAT), bf),
        pltpu.VMEM((4, HALF, FEAT), bf),
        pltpu.VMEM((4, HALF, FEAT), bf),
        pltpu.VMEM((4, HALF, FEAT), bf),
        pltpu.VMEM((4, BLK, FEAT), f32),
        pltpu.VMEM((4, BLK, FEAT), bf),
        pltpu.VMEM((4, BLK, FEAT), bf),
        pltpu.VMEM((EXPERTS, 8, FEAT + 128), f32),
        pltpu.VMEM((EXPERTS, 8, FEAT + 128), f32),
        pltpu.VMEM((NZ, 8, 128), f32),
        pltpu.VMEM((4, 8, 128), f32),
        pltpu.VMEM((8, 128), f32),
        dma((5,)), dma((3,)),
        dma((3,)), dma((3,)),
        dma((8,)), dma((8,)),
        dma((4,)), dma((4,)),
        dma((4, 2)), dma((4, 2)),
        dma((4, 2)), dma((4, 2)),
        dma((4,)), dma((4,)),
        dma((4,)), dma((4,)),
        dma((4,)), dma((4,)),
        dma((8,)), dma((8,)),
        dma((8,)), dma((8,)),
        dma((4,)), dma((4,)),
    ]
    d_tok, d_gate = pl.pallas_call(
        kernel,
        out_shape=(
            jax.ShapeDtypeStruct((TOK, FEAT), bf),
            jax.ShapeDtypeStruct((2, TOK), f32),
        ),
        in_specs=[hbm] * 8,
        out_specs=(vmem, vmem),
        scratch_shapes=scratch,
        name="moe_dx",
        compiler_params=pltpu.CompilerParams(
            collective_id=0, has_side_effects=True, vmem_limit_bytes=60 * 2**20
        ),
        cost_estimate=pl.CostEstimate(
            flops=5 * 2 * HALF * NZ * FEAT * 2 * HID, bytes_accessed=6 * NZ * FEAT * HID, transcendentals=HALF * 2 * HID
        ),
    )(tokens_in, d_out, gates.T, expert_ids.T, slot_ids.T, w_gate, w_up, w_down)
    return d_tok, d_gate.T


def solution(mesh):
    placed = (
        P("ep", "tp"),
        P("ep", "tp"),
        P("ep", None),
        P("ep", None),
        P("ep", None),
        P(None, ("ep", "tp")),
        P(None, ("ep", "tp")),
        P(("ep", "tp"), None),
    )
    return jax.shard_map(
        local, mesh=mesh, in_specs=placed, out_specs=(P("ep", "tp"), P("ep", None)), check_vma=False
    )
```

```python
import jax
import jax.numpy as jnp
from jax import lax
from jax.experimental import pallas as pl
from jax.experimental.pallas import tpu as pltpu
from jax.sharding import PartitionSpec as P

MESH = pl.DeviceIdType.MESH
HIGH = lax.Precision.HIGHEST
EXPERTS = 8
CAP = 6
TOK = 16
NZ = 8
FEAT = 384
HID = 256
BLK = 48
HALF = 192
PR = 32
QR = BLK - PR
PALL = 4 * PR


def iota(shape, dim):
    return lax.broadcasted_iota(jnp.int32, shape, dim)


def div6(v):
    return (v * 43) >> 8


def row_of(r):
    q = r - PALL
    first = r < PALL
    return jnp.where(first, r >> 5, q >> 4), jnp.where(first, r & (PR - 1), PR + (q & (QR - 1)))


def kernel(
    tok_h, dout_h, gates_h, ids_h, slots_h, wg, wu, wd, d_tok, d_gate,
    tok, dout, gates, ids, slots, wgu, wdn, send, drecv, G, acc_gu, acc_b, gcat, part,
    rsend, rrecv, lsend, lrecv, total, ysend, yrecv, ret, back, scz, scy, scs,
    i_sem, w_sem, p_ss, p_rs, d_ss, d_rs, y_ss, y_rs, q_ss, q_rs, qz_ss, qz_rs, r_ss, r_rs, l_ss, l_rs,
    rr_ss, rr_rs, rl_ss, rl_rs, yy_ss, yy_rs, t_ss, t_rs, z_ss, z_rs, s_ss, s_rs,
):
    ep = lax.axis_index("ep")
    z = lax.axis_index("tp")
    own = lax.div(ep, 8)
    place = lax.rem(ep, 8)
    yl = lax.div(place, 2)
    c = lax.rem(place, 2)

    def at_expert(e):
        mirrored = lax.rem(own + e, 2)
        return (e * 8 + (yl + mirrored * (3 - 2 * yl)) * 2 + c, z)

    def at_y(yy):
        return (own * 8 + yy * 2 + c, z)

    def at_z(zz):
        return (ep, zz)

    sibling = (own * 8 + yl * 2 + 1 - c, z)

    def copy(src, dst, ss, rs, dev):
        return pltpu.make_async_remote_copy(
            src_ref=src, dst_ref=dst, send_sem=ss, recv_sem=rs, device_id=dev, device_id_type=MESH
        )

    waits = []

    def start(cp):
        cp.start()
        waits.append(cp)

    def weights(core):
        at = pl.multiple_of(core * HID, HID)
        return (
            (wg, wgu.at[:, pl.ds(at, HID)]),
            (wu, wgu.at[:, pl.ds(pl.multiple_of(at + 2 * HID, HID), HID)]),
            (wd, wdn.at[pl.ds(at, HID), :]),
        )

    small = [
        pltpu.make_async_copy(src, dst, i_sem.at[i])
        for i, (src, dst) in enumerate(
            ((ids_h, ids), (slots_h, slots), (tok_h, tok), (dout_h, dout), (gates_h, gates))
        )
    ]
    loads = [
        pltpu.make_async_copy(src, dst, w_sem.at[i]) for i, (src, dst) in enumerate(weights(c))
    ]
    for ld in small + loads:
        ld.start()

    barrier = pltpu.get_barrier_semaphore()
    peers = [at_expert(lax.rem(own + i, 8)) for i in range(1, 8)]
    peers += [at_y(lax.rem(yl + i, 4)) for i in range(1, 4)]
    peers += [at_z(lax.rem(z + i, NZ)) for i in range(1, NZ)]
    peers += [sibling]
    for dev in peers:
        pl.semaphore_signal(barrier, inc=1, device_id=dev, device_id_type=MESH)

    for ld in small:
        ld.wait()
    r = iota((128, TOK), 0)
    pick = jnp.zeros((128, TOK), jnp.float32)
    for k in range(2):
        hit = (ids[k : k + 1, :] == (r >> 4)) & (slots[k : k + 1, :] == (r & 7))
        pick = pick + hit.astype(jnp.float32)
    is_back = (r & 8) == 8
    pick_in = jnp.where(is_back, 0.0, pick).astype(jnp.bfloat16)
    pick_back = jnp.where(is_back, pick, 0.0).astype(jnp.bfloat16)
    placed = jnp.dot(pick_in, tok[...], preferred_element_type=jnp.float32)
    placed = placed + jnp.dot(pick_back, dout[...], preferred_element_type=jnp.float32)
    send[...] = placed.astype(jnp.bfloat16).reshape(EXPERTS, 16, FEAT)

    pl.semaphore_wait(barrier, len(peers))

    for i in range(1, 8):
        e = lax.rem(own + i, 8)
        start(copy(send.at[e], drecv.at[own], d_ss.at[i], d_rs.at[i], at_expert(e)))
    for i, (src, dst) in enumerate(weights(c)):
        start(copy(src, dst, p_ss.at[i], p_rs.at[i], sibling))
    drecv[own] = send[own]
    r = iota((2 * BLK, 128), 0)
    second = (r >= BLK).astype(jnp.int32)
    q = r - second * BLK
    j6 = div6(q)
    sel = (iota((2 * BLK, 128), 1) == j6 * 16 + second * 8 + (q - 6 * j6)).astype(jnp.bfloat16)
    for i in range(1, 8):
        j = lax.rem(own + 8 - i, 8)
        copy(send.at[j], drecv.at[j], d_ss.at[i], d_rs.at[i], at_expert(j)).wait_recv()
    dense = jnp.dot(sel, drecv[...].reshape(128, FEAT), preferred_element_type=jnp.float32)
    dense = dense.astype(jnp.bfloat16)
    p_rows = pl.ds(pl.multiple_of(yl * PR, PR), PR)
    q_rows = pl.ds(pl.multiple_of(PALL + yl * QR, QR), QR)
    for a in range(2):
        G[z, a, p_rows, :] = dense[a * BLK : a * BLK + PR]
        G[z, a, q_rows, :] = dense[a * BLK + PR : (a + 1) * BLK]

    def slot_of(n):
        if n == 0:
            return z
        if n <= 3:
            return lax.rem(z + NZ - n, NZ)
        if n <= 6:
            return lax.rem(z + n - 3, NZ)
        return lax.rem(z + 4, NZ)

    z_right, z_left = at_z(lax.rem(z + 1, NZ)), at_z(lax.rem(z + NZ - 1, NZ))

    def q_own(i):
        blk = G.at[z, :, q_rows]
        return copy(blk, blk, qz_ss.at[i], qz_rs.at[i], at_z(lax.rem(z + i, NZ)))

    def q_from(i):
        zz = lax.rem(z + NZ - i, NZ)
        blk = G.at[zz, :, q_rows]
        return copy(blk, blk, qz_ss.at[i], qz_rs.at[i], at_z(zz))

    def q_spread(n):
        blk = G.at[slot_of(n), :, q_rows]
        for i in range(1, 4):
            start(copy(blk, blk, q_ss.at[n, i], q_rs.at[n, i], at_y(lax.rem(yl + i, 4))))

    def q_got(n):
        for i in range(1, 4):
            yy = lax.rem(yl + 4 - i, 4)
            blk = G.at[slot_of(n), :, pl.ds(pl.multiple_of(PALL + yy * QR, QR), QR)]
            copy(blk, blk, q_ss.at[n, i], q_rs.at[n, i], at_y(yy)).wait_recv()

    def over_y(i, yy, dev):
        blk = G.at[z, :, pl.ds(pl.multiple_of(yy * PR, PR), PR)]
        return copy(blk, blk, y_ss.at[i], y_rs.at[i], dev)

    def right(k, a, shift=0):
        blk = G.at[lax.rem(z + NZ - k - shift, NZ), a, pl.ds(0, PALL)]
        return copy(blk, blk, r_ss.at[k, a], r_rs.at[k, a], z_right)

    def left(k, a, shift=0):
        blk = G.at[lax.rem(z + k + shift, NZ), a, pl.ds(0, PALL)]
        return copy(blk, blk, l_ss.at[k, a], l_rs.at[k, a], z_left)

    def p_step(k):
        for a in range(2):
            if k < 3 or a == 0:
                right(k, a, 1).wait_recv()
                if k < 2 or (k == 2 and a == 0):
                    start(right(k + 1, a))
            if k < 3 or a == 1:
                left(k, a, 1).wait_recv()
                if k < 2 or (k == 2 and a == 1):
                    start(left(k + 1, a))

    def products(n):
        q_got(n)
        slot = slot_of(n)
        base = pl.multiple_of(slot * FEAT, FEAT)
        acc_gu[...] += jnp.dot(
            G[slot, 0], wgu[pl.ds(base, FEAT), :], preferred_element_type=jnp.float32
        )
        acc_b[...] += lax.dot_general(
            G[slot, 1], wdn[:, pl.ds(base, FEAT)], (((1,), (1,)), ((), ())),
            preferred_element_type=jnp.float32,
        )

    near = (1, 7, 2, 6, 3, 5, 4)
    for i in near:
        start(q_own(i))
    for i in range(1, 4):
        yy = lax.rem(yl + i, 4)
        start(over_y(i, yl, at_y(yy)))
    q_spread(0)
    acc_gu[...] = jnp.zeros_like(acc_gu)
    acc_b[...] = jnp.zeros_like(acc_b)
    for i in range(1, 4):
        yy = lax.rem(yl + 4 - i, 4)
        over_y(i, yy, at_y(yy)).wait_recv()
    for a in range(2):
        start(right(0, a))
        start(left(0, a))
    for i in near:
        q_from(i).wait_recv()
        q_spread(i if i <= 3 else 7 if i == 4 else 11 - i)
    for ld in loads:
        ld.wait()
    for i, (src, dst) in enumerate(weights(1 - c)):
        copy(src, dst, p_ss.at[i], p_rs.at[i], sibling).wait_recv()
    p_step(0)
    products(0)
    p_step(1)
    products(1)
    products(4)
    p_step(2)
    products(2)
    products(5)
    products(3)
    products(6)
    p_step(3)
    products(7)

    parts = (pl.ds(0, PALL), pl.ds(PALL, HALF - PALL))

    def hidden(h):
        gate = acc_gu[parts[h], : 2 * HID]
        up = acc_gu[parts[h], 2 * HID :]
        bg = acc_b[parts[h], :]
        sg = jax.nn.sigmoid(gate)
        silu = gate * sg
        gcat[parts[h], : 2 * HID] = (bg * up * sg * (1.0 + gate * (1.0 - sg))).astype(jnp.bfloat16)
        gcat[parts[h], 2 * HID :] = (bg * silu).astype(jnp.bfloat16)
        return jnp.sum(silu * up * bg, axis=1, keepdims=True)

    def slice_grad(slot, rows):
        base = pl.multiple_of(slot * FEAT, FEAT)
        part[slot, rows, :] = lax.dot_general(
            gcat[rows, :], wgu[pl.ds(base, FEAT), :], (((1,), (1,)), ((), ())),
            preferred_element_type=jnp.float32,
        )

    def ring_r(k, h):
        return copy(
            rsend.at[k, parts[h]], rrecv.at[k, parts[h]], rr_ss.at[k, h], rr_rs.at[k, h], z_right
        )

    def ring_l(k, h):
        return copy(
            lsend.at[k, parts[h]], lrecv.at[k, parts[h]], rl_ss.at[k, h], rl_rs.at[k, h], z_left
        )

    far = slot_of(7)
    score0 = hidden(0)
    slice_grad(far, parts[0])
    rsend[0, parts[0], :] = part[far, parts[0], :].astype(jnp.bfloat16)
    start(ring_r(0, 0))
    score1 = hidden(1)
    slice_grad(far, parts[1])
    lsend[0, parts[1], :] = part[far, parts[1], :].astype(jnp.bfloat16)
    start(ring_l(0, 1))
    score = jnp.concatenate([score0, score1], axis=0)

    q = row_of(iota((HALF, 128), 0))[1]
    j6 = div6(q)
    spread = jnp.where(iota((HALF, 128), 1) == j6 * 8 + (q - 6 * j6), score, 0.0)
    mine = (row_of(iota((8, HALF), 1))[0] == iota((8, HALF), 0)).astype(jnp.float32)
    scz[z] = jnp.dot(mine, spread, precision=HIGH, preferred_element_type=jnp.float32)
    for i in range(1, NZ):
        start(copy(scz.at[z], scz.at[z], z_ss.at[i], z_rs.at[i], at_z(lax.rem(z + i, NZ))))

    for k in range(1, 4):
        nr, nl = slot_of(7 - k), slot_of(4 - k)
        slice_grad(nr, pl.ds(0, HALF))
        slice_grad(nl, pl.ds(0, HALF))
        for h, ring, slot, out, got in (
            (1, ring_r, nr, rsend, rrecv),
            (0, ring_l, nl, lsend, lrecv),
            (0, ring_r, nr, rsend, rrecv),
            (1, ring_l, nl, lsend, lrecv),
        ):
            term = part[slot, parts[h], :]
            if k > 1 or (h == 0) == (out is rsend):
                ring(k - 1, h).wait_recv()
                term = term + got[k - 1, parts[h], :].astype(jnp.float32)
            out[k, parts[h], :] = term.astype(jnp.bfloat16)
            start(ring(k, h))
        if k == 2:
            for i in range(1, NZ):
                zz = lax.rem(z + NZ - i, NZ)
                copy(scz.at[zz], scz.at[zz], z_ss.at[i], z_rs.at[i], at_z(zz)).wait_recv()
            scy[yl] = jnp.sum(scz[...], axis=0)
            for i in range(1, 4):
                yy = lax.rem(yl + i, 4)
                start(copy(scy.at[yl], scy.at[yl], s_ss.at[i], s_rs.at[i], at_y(yy)))
    slice_grad(z, pl.ds(0, HALF))
    for i in range(1, 4):
        yy = lax.rem(yl + 4 - i, 4)
        copy(scy.at[yy], scy.at[yy], s_ss.at[i], s_rs.at[i], at_y(yy)).wait_recv()
    scs[...] = jnp.sum(scy[...], axis=0)
    places = (pl.ds(0, PR), pl.ds(PR, QR))
    for h, size in ((1, QR), (0, PR)):
        ring_r(3, h).wait_recv()
        ring_l(3, h).wait_recv()
        summed = part[z, parts[h], :] + rrecv[3, parts[h], :].astype(jnp.float32)
        summed = summed + lrecv[3, parts[h], :].astype(jnp.float32)
        total[parts[h], :] = summed
        ysend[:, places[h], :] = summed.astype(jnp.bfloat16).reshape(4, size, FEAT)
        for i in range(1, 4):
            yy = lax.rem(yl + i, 4)
            start(
                copy(
                    ysend.at[yy, places[h]], yrecv.at[i, places[h]],
                    yy_ss.at[i, h], yy_rs.at[i, h], at_y(yy),
                )
            )
    rows = jnp.concatenate([total[p_rows, :], total[q_rows, :]], axis=0)
    for i in range(1, 4):
        for h in (1, 0):
            dst = yrecv.at[i, places[h]]
            copy(dst, dst, yy_ss.at[i, h], yy_rs.at[i, h], at_y(lax.rem(yl + 4 - i, 4))).wait_recv()
        rows = rows + yrecv[i].astype(jnp.float32)

    r = iota((64, BLK), 0)
    pos = iota((64, BLK), 1)
    sel = (((r & 7) < CAP) & (pos == (r >> 3) * 6 + (r & 7))).astype(jnp.float32)
    ret[:, :, :FEAT] = jnp.dot(
        sel, rows, precision=HIGH, preferred_element_type=jnp.float32
    ).reshape(EXPERTS, 8, FEAT)
    ret[:, :, FEAT:] = jnp.broadcast_to(scs[...][None], (EXPERTS, 8, 128))
    for i in range(1, 8):
        e = lax.rem(own + i, 8)
        start(copy(ret.at[e], back.at[own], t_ss.at[i], t_rs.at[i], at_expert(e)))
    back[own] = ret[own]
    r = iota((64, TOK), 0)
    hits = []
    weight = jnp.zeros((64, TOK), jnp.float32)
    for k in range(2):
        hit = (ids[k : k + 1, :] == (r >> 3)) & (slots[k : k + 1, :] == (r & 7))
        hits.append(hit)
        weight = weight + jnp.where(hit, gates[k : k + 1, :], 0.0)
    for i in range(1, 8):
        j = lax.rem(own + 8 - i, 8)
        copy(ret.at[j], back.at[j], t_ss.at[i], t_rs.at[i], at_expert(j)).wait_recv()
    d_tok[...] = lax.dot_general(
        weight, back[:, :, :FEAT].reshape(64, FEAT), (((0,), (0,)), ((), ())),
        precision=HIGH, preferred_element_type=jnp.float32,
    ).astype(jnp.bfloat16)
    sc = back[:, :, FEAT:]
    same = lax.rem(iota((EXPERTS, 8, 128), 0) + own, 2) == 0
    row = jnp.where(same, yl, 3 - yl)
    sc = jnp.sum(jnp.where(iota((EXPERTS, 8, 128), 1) == row, sc, 0.0), axis=1, keepdims=True)
    sc = jnp.broadcast_to(sc, (EXPERTS, 8, 128)).reshape(64, 128)
    lane = own * 8 + (iota((64, 128), 0) & 7)
    sc = jnp.sum(jnp.where(iota((64, 128), 1) == lane, sc, 0.0), axis=1, keepdims=True)
    for k in range(2):
        d_gate[k : k + 1, :] = jnp.sum(jnp.where(hits[k], sc, 0.0), axis=0, keepdims=True)
    for cp in waits:
        cp.wait_send()


def local(tokens_in, d_out, gates, expert_ids, slot_ids, w_gate, w_up, w_down):
    vmem = pl.BlockSpec(memory_space=pltpu.VMEM)
    hbm = pl.BlockSpec(memory_space=pltpu.HBM)
    bf, f32, dma = jnp.bfloat16, jnp.float32, pltpu.SemaphoreType.DMA
    scratch = [
        pltpu.VMEM((TOK, FEAT), bf),
        pltpu.VMEM((TOK, FEAT), bf),
        pltpu.VMEM((2, TOK), f32),
        pltpu.VMEM((2, TOK), jnp.int32),
        pltpu.VMEM((2, TOK), jnp.int32),
        pltpu.VMEM((NZ * FEAT, 4 * HID), bf),
        pltpu.VMEM((2 * HID, NZ * FEAT), bf),
        pltpu.VMEM((EXPERTS, 16, FEAT), bf),
        pltpu.VMEM((EXPERTS, 16, FEAT), bf),
        pltpu.VMEM((NZ, 2, HALF, FEAT), bf),
        pltpu.VMEM((HALF, 4 * HID), f32),
        pltpu.VMEM((HALF, 2 * HID), f32),
        pltpu.VMEM((HALF, 4 * HID), bf),
        pltpu.VMEM((NZ, HALF, FEAT), f32),
        pltpu.VMEM((4, HALF, FEAT), bf),
        pltpu.VMEM((4, HALF, FEAT), bf),
        pltpu.VMEM((4, HALF, FEAT), bf),
        pltpu.VMEM((4, HALF, FEAT), bf),
        pltpu.VMEM((HALF, FEAT), f32),
        pltpu.VMEM((4, BLK, FEAT), bf),
        pltpu.VMEM((4, BLK, FEAT), bf),
        pltpu.VMEM((EXPERTS, 8, FEAT + 128), f32),
        pltpu.VMEM((EXPERTS, 8, FEAT + 128), f32),
        pltpu.VMEM((NZ, 8, 128), f32),
        pltpu.VMEM((4, 8, 128), f32),
        pltpu.VMEM((8, 128), f32),
        dma((5,)), dma((3,)),
        dma((3,)), dma((3,)),
        dma((8,)), dma((8,)),
        dma((4,)), dma((4,)),
        dma((8, 4)), dma((8, 4)),
        dma((8,)), dma((8,)),
        dma((4, 2)), dma((4, 2)),
        dma((4, 2)), dma((4, 2)),
        dma((4, 2)), dma((4, 2)),
        dma((4, 2)), dma((4, 2)),
        dma((4, 2)), dma((4, 2)),
        dma((8,)), dma((8,)),
        dma((8,)), dma((8,)),
        dma((4,)), dma((4,)),
    ]
    d_tok, d_gate = pl.pallas_call(
        kernel,
        out_shape=(
            jax.ShapeDtypeStruct((TOK, FEAT), bf),
            jax.ShapeDtypeStruct((2, TOK), f32),
        ),
        in_specs=[hbm] * 8,
        out_specs=(vmem, vmem),
        scratch_shapes=scratch,
        name="moe_dx",
        compiler_params=pltpu.CompilerParams(
            collective_id=0, has_side_effects=True, vmem_limit_bytes=60 * 2**20
        ),
        cost_estimate=pl.CostEstimate(
            flops=5 * 2 * HALF * NZ * FEAT * 2 * HID, bytes_accessed=6 * NZ * FEAT * HID, transcendentals=HALF * 2 * HID
        ),
    )(tokens_in, d_out, gates.T, expert_ids.T, slot_ids.T, w_gate, w_up, w_down)
    return d_tok, d_gate.T


def solution(mesh):
    placed = (
        P("ep", "tp"),
        P("ep", "tp"),
        P("ep", None),
        P("ep", None),
        P("ep", None),
        P(None, ("ep", "tp")),
        P(None, ("ep", "tp")),
        P(("ep", "tp"), None),
    )
    return jax.shard_map(
        local, mesh=mesh, in_specs=placed, out_specs=(P("ep", "tp"), P("ep", None)), check_vma=False
    )
```

```python
import jax
import jax.numpy as jnp
from jax import lax
from jax.experimental import pallas as pl
from jax.experimental.pallas import tpu as pltpu
from jax.sharding import PartitionSpec as P

MESH = pl.DeviceIdType.MESH
HIGH = lax.Precision.HIGHEST
EXPERTS = 8
CAP = 6
TOK = 16
NZ = 8
FEAT = 384
HID = 256
BLK = 48
HALF = 192
PR = 32
QR = BLK - PR
PALL = 4 * PR


def iota(shape, dim):
    return lax.broadcasted_iota(jnp.int32, shape, dim)


def div6(v):
    return (v * 43) >> 8


def row_of(r):
    q = r - PALL
    first = r < PALL
    return jnp.where(first, r >> 5, q >> 4), jnp.where(first, r & (PR - 1), PR + (q & (QR - 1)))


def kernel(
    tok_h, dout_h, gates_h, ids_h, slots_h, wg, wu, wd, d_tok, d_gate,
    tok, dout, gates, ids, slots, wgu, wdn, send, drecv, G, acc_gu, acc_b, gcat, part,
    rsend, rrecv, lsend, lrecv, total, ysend, yrecv, ret, back, scz, scy, scs,
    i_sem, w_sem, p_ss, p_rs, d_ss, d_rs, y_ss, y_rs, q_ss, q_rs, qz_ss, qz_rs, r_ss, r_rs, l_ss, l_rs,
    rr_ss, rr_rs, rl_ss, rl_rs, yy_ss, yy_rs, t_ss, t_rs, z_ss, z_rs, s_ss, s_rs,
):
    ep = lax.axis_index("ep")
    z = lax.axis_index("tp")
    own = lax.div(ep, 8)
    place = lax.rem(ep, 8)
    yl = lax.div(place, 2)
    c = lax.rem(place, 2)

    def at_expert(e):
        mirrored = lax.rem(own + e, 2)
        return (e * 8 + (yl + mirrored * (3 - 2 * yl)) * 2 + lax.rem(c + z, 2), z)

    def at_y(yy):
        return (own * 8 + yy * 2 + c, z)

    def at_z(zz):
        return (own * 8 + yl * 2 + lax.rem(c + z + zz, 2), zz)

    sibling = (own * 8 + yl * 2 + 1 - c, z)

    def copy(src, dst, ss, rs, dev):
        return pltpu.make_async_remote_copy(
            src_ref=src, dst_ref=dst, send_sem=ss, recv_sem=rs, device_id=dev, device_id_type=MESH
        )

    waits = []

    def start(cp):
        cp.start()
        waits.append(cp)

    def weights(core):
        at = pl.multiple_of(core * HID, HID)
        return (
            (wg, wgu.at[:, pl.ds(at, HID)]),
            (wu, wgu.at[:, pl.ds(pl.multiple_of(at + 2 * HID, HID), HID)]),
            (wd, wdn.at[pl.ds(at, HID), :]),
        )

    small = [
        pltpu.make_async_copy(src, dst, i_sem.at[i])
        for i, (src, dst) in enumerate(
            ((ids_h, ids), (slots_h, slots), (tok_h, tok), (dout_h, dout), (gates_h, gates))
        )
    ]
    loads = [
        pltpu.make_async_copy(src, dst, w_sem.at[i]) for i, (src, dst) in enumerate(weights(c))
    ]
    for ld in small + loads:
        ld.start()

    barrier = pltpu.get_barrier_semaphore()
    peers = [at_expert(lax.rem(own + i, 8)) for i in range(1, 8)]
    peers += [at_y(lax.rem(yl + i, 4)) for i in range(1, 4)]
    peers += [at_z(lax.rem(z + i, NZ)) for i in range(1, NZ)]
    peers += [sibling]
    for dev in peers:
        pl.semaphore_signal(barrier, inc=1, device_id=dev, device_id_type=MESH)

    for ld in small:
        ld.wait()
    r = iota((128, TOK), 0)
    pick = jnp.zeros((128, TOK), jnp.float32)
    for k in range(2):
        hit = (ids[k : k + 1, :] == (r >> 4)) & (slots[k : k + 1, :] == (r & 7))
        pick = pick + hit.astype(jnp.float32)
    is_back = (r & 8) == 8
    pick_in = jnp.where(is_back, 0.0, pick).astype(jnp.bfloat16)
    pick_back = jnp.where(is_back, pick, 0.0).astype(jnp.bfloat16)
    placed = jnp.dot(pick_in, tok[...], preferred_element_type=jnp.float32)
    placed = placed + jnp.dot(pick_back, dout[...], preferred_element_type=jnp.float32)
    send[...] = placed.astype(jnp.bfloat16).reshape(EXPERTS, 16, FEAT)

    pl.semaphore_wait(barrier, len(peers))

    for i in range(1, 8):
        e = lax.rem(own + i, 8)
        start(copy(send.at[e], drecv.at[own], d_ss.at[i], d_rs.at[i], at_expert(e)))
    for i, (src, dst) in enumerate(weights(c)):
        start(copy(src, dst, p_ss.at[i], p_rs.at[i], sibling))
    @pl.when(lax.rem(z, 2) == 0)
    def _():
        drecv[own] = send[own]

    @pl.when(lax.rem(z, 2) == 1)
    def _():
        copy(send.at[own], drecv.at[own], d_ss.at[0], d_rs.at[0], sibling).start()

    r = iota((2 * BLK, 128), 0)
    second = (r >= BLK).astype(jnp.int32)
    q = r - second * BLK
    j6 = div6(q)
    sel = (iota((2 * BLK, 128), 1) == j6 * 16 + second * 8 + (q - 6 * j6)).astype(jnp.bfloat16)
    for i in range(1, 8):
        j = lax.rem(own + 8 - i, 8)
        copy(send.at[j], drecv.at[j], d_ss.at[i], d_rs.at[i], at_expert(j)).wait_recv()

    @pl.when(lax.rem(z, 2) == 1)
    def _():
        copy(send.at[own], drecv.at[own], d_ss.at[0], d_rs.at[0], sibling).wait()

    dense = jnp.dot(sel, drecv[...].reshape(128, FEAT), preferred_element_type=jnp.float32)
    dense = dense.astype(jnp.bfloat16)
    p_rows = pl.ds(pl.multiple_of(yl * PR, PR), PR)
    q_rows = pl.ds(pl.multiple_of(PALL + yl * QR, QR), QR)
    for a in range(2):
        G[z, a, p_rows, :] = dense[a * BLK : a * BLK + PR]
        G[z, a, q_rows, :] = dense[a * BLK + PR : (a + 1) * BLK]

    def slot_of(n):
        if n == 0:
            return z
        if n <= 3:
            return lax.rem(z + NZ - n, NZ)
        if n <= 6:
            return lax.rem(z + n - 3, NZ)
        return lax.rem(z + 4, NZ)

    z_right, z_left = at_z(lax.rem(z + 1, NZ)), at_z(lax.rem(z + NZ - 1, NZ))

    def q_own(i):
        blk = G.at[z, :, q_rows]
        return copy(blk, blk, qz_ss.at[i], qz_rs.at[i], at_z(lax.rem(z + i, NZ)))

    def q_from(i):
        zz = lax.rem(z + NZ - i, NZ)
        blk = G.at[zz, :, q_rows]
        return copy(blk, blk, qz_ss.at[i], qz_rs.at[i], at_z(zz))

    def q_spread(n):
        blk = G.at[slot_of(n), :, q_rows]
        for i in range(1, 4):
            start(copy(blk, blk, q_ss.at[n, i], q_rs.at[n, i], at_y(lax.rem(yl + i, 4))))

    def q_got(n):
        for i in range(1, 4):
            yy = lax.rem(yl + 4 - i, 4)
            blk = G.at[slot_of(n), :, pl.ds(pl.multiple_of(PALL + yy * QR, QR), QR)]
            copy(blk, blk, q_ss.at[n, i], q_rs.at[n, i], at_y(yy)).wait_recv()

    def over_y(i, yy, dev):
        blk = G.at[z, :, pl.ds(pl.multiple_of(yy * PR, PR), PR)]
        return copy(blk, blk, y_ss.at[i], y_rs.at[i], dev)

    def right(k, a, shift=0):
        blk = G.at[lax.rem(z + NZ - k - shift, NZ), a, pl.ds(0, PALL)]
        return copy(blk, blk, r_ss.at[k, a], r_rs.at[k, a], z_right)

    def left(k, a, shift=0):
        blk = G.at[lax.rem(z + k + shift, NZ), a, pl.ds(0, PALL)]
        return copy(blk, blk, l_ss.at[k, a], l_rs.at[k, a], z_left)

    def p_step(k):
        for a in range(2):
            if k < 3 or a == 0:
                right(k, a, 1).wait_recv()
                if k < 2 or (k == 2 and a == 0):
                    start(right(k + 1, a))
            if k < 3 or a == 1:
                left(k, a, 1).wait_recv()
                if k < 2 or (k == 2 and a == 1):
                    start(left(k + 1, a))

    def products(n):
        q_got(n)
        slot = slot_of(n)
        base = pl.multiple_of(slot * FEAT, FEAT)
        acc_gu[...] += jnp.dot(
            G[slot, 0], wgu[pl.ds(base, FEAT), :], preferred_element_type=jnp.float32
        )
        acc_b[...] += lax.dot_general(
            G[slot, 1], wdn[:, pl.ds(base, FEAT)], (((1,), (1,)), ((), ())),
            preferred_element_type=jnp.float32,
        )

    near = (1, 7, 2, 6, 3, 5, 4)
    for i in near:
        start(q_own(i))
    for i in range(1, 4):
        yy = lax.rem(yl + i, 4)
        start(over_y(i, yl, at_y(yy)))
    q_spread(0)
    acc_gu[...] = jnp.zeros_like(acc_gu)
    acc_b[...] = jnp.zeros_like(acc_b)
    for i in range(1, 4):
        yy = lax.rem(yl + 4 - i, 4)
        over_y(i, yy, at_y(yy)).wait_recv()
    for a in range(2):
        start(right(0, a))
        start(left(0, a))
    for i in near:
        q_from(i).wait_recv()
        q_spread(i if i <= 3 else 7 if i == 4 else 11 - i)
    for ld in loads:
        ld.wait()
    for i, (src, dst) in enumerate(weights(1 - c)):
        copy(src, dst, p_ss.at[i], p_rs.at[i], sibling).wait_recv()
    p_step(0)
    products(0)
    p_step(1)
    products(1)
    products(4)
    p_step(2)
    products(2)
    products(5)
    products(3)
    products(6)
    p_step(3)
    products(7)

    parts = (pl.ds(0, PALL), pl.ds(PALL, HALF - PALL))

    def hidden(h):
        gate = acc_gu[parts[h], : 2 * HID]
        up = acc_gu[parts[h], 2 * HID :]
        bg = acc_b[parts[h], :]
        sg = jax.nn.sigmoid(gate)
        silu = gate * sg
        gcat[parts[h], : 2 * HID] = (bg * up * sg * (1.0 + gate * (1.0 - sg))).astype(jnp.bfloat16)
        gcat[parts[h], 2 * HID :] = (bg * silu).astype(jnp.bfloat16)
        return jnp.sum(silu * up * bg, axis=1, keepdims=True)

    def slice_grad(slot, rows):
        base = pl.multiple_of(slot * FEAT, FEAT)
        part[slot, rows, :] = lax.dot_general(
            gcat[rows, :], wgu[pl.ds(base, FEAT), :], (((1,), (1,)), ((), ())),
            preferred_element_type=jnp.float32,
        )

    def ring_r(k, h):
        return copy(
            rsend.at[k, parts[h]], rrecv.at[k, parts[h]], rr_ss.at[k, h], rr_rs.at[k, h], z_right
        )

    def ring_l(k, h):
        return copy(
            lsend.at[k, parts[h]], lrecv.at[k, parts[h]], rl_ss.at[k, h], rl_rs.at[k, h], z_left
        )

    far = slot_of(7)
    score0 = hidden(0)
    slice_grad(far, parts[0])
    rsend[0, parts[0], :] = part[far, parts[0], :].astype(jnp.bfloat16)
    start(ring_r(0, 0))
    score1 = hidden(1)
    slice_grad(far, parts[1])
    lsend[0, parts[1], :] = part[far, parts[1], :].astype(jnp.bfloat16)
    start(ring_l(0, 1))
    score = jnp.concatenate([score0, score1], axis=0)

    q = row_of(iota((HALF, 128), 0))[1]
    j6 = div6(q)
    spread = jnp.where(iota((HALF, 128), 1) == j6 * 8 + (q - 6 * j6), score, 0.0)
    mine = (row_of(iota((8, HALF), 1))[0] == iota((8, HALF), 0)).astype(jnp.float32)
    scz[z] = jnp.dot(mine, spread, precision=HIGH, preferred_element_type=jnp.float32)
    for i in range(1, NZ):
        start(copy(scz.at[z], scz.at[z], z_ss.at[i], z_rs.at[i], at_z(lax.rem(z + i, NZ))))

    for k in range(1, 4):
        nr, nl = slot_of(7 - k), slot_of(4 - k)
        slice_grad(nr, pl.ds(0, HALF))
        slice_grad(nl, pl.ds(0, HALF))
        for h, ring, slot, out, got in (
            (1, ring_r, nr, rsend, rrecv),
            (0, ring_l, nl, lsend, lrecv),
            (0, ring_r, nr, rsend, rrecv),
            (1, ring_l, nl, lsend, lrecv),
        ):
            term = part[slot, parts[h], :]
            if k > 1 or (h == 0) == (out is rsend):
                ring(k - 1, h).wait_recv()
                term = term + got[k - 1, parts[h], :].astype(jnp.float32)
            out[k, parts[h], :] = term.astype(jnp.bfloat16)
            start(ring(k, h))
        if k == 2:
            for i in range(1, NZ):
                zz = lax.rem(z + NZ - i, NZ)
                copy(scz.at[zz], scz.at[zz], z_ss.at[i], z_rs.at[i], at_z(zz)).wait_recv()
            scy[yl] = jnp.sum(scz[...], axis=0)
            for i in range(1, 4):
                yy = lax.rem(yl + i, 4)
                start(copy(scy.at[yl], scy.at[yl], s_ss.at[i], s_rs.at[i], at_y(yy)))
    slice_grad(z, pl.ds(0, HALF))
    for i in range(1, 4):
        yy = lax.rem(yl + 4 - i, 4)
        copy(scy.at[yy], scy.at[yy], s_ss.at[i], s_rs.at[i], at_y(yy)).wait_recv()
    scs[...] = jnp.sum(scy[...], axis=0)
    places = (pl.ds(0, PR), pl.ds(PR, QR))
    for h, size in ((1, QR), (0, PR)):
        ring_r(3, h).wait_recv()
        ring_l(3, h).wait_recv()
        summed = part[z, parts[h], :] + rrecv[3, parts[h], :].astype(jnp.float32)
        summed = summed + lrecv[3, parts[h], :].astype(jnp.float32)
        total[parts[h], :] = summed
        ysend[:, places[h], :] = summed.astype(jnp.bfloat16).reshape(4, size, FEAT)
        for i in range(1, 4):
            yy = lax.rem(yl + i, 4)
            start(
                copy(
                    ysend.at[yy, places[h]], yrecv.at[i, places[h]],
                    yy_ss.at[i, h], yy_rs.at[i, h], at_y(yy),
                )
            )
    rows = jnp.concatenate([total[p_rows, :], total[q_rows, :]], axis=0)
    for i in range(1, 4):
        for h in (1, 0):
            dst = yrecv.at[i, places[h]]
            copy(dst, dst, yy_ss.at[i, h], yy_rs.at[i, h], at_y(lax.rem(yl + 4 - i, 4))).wait_recv()
        rows = rows + yrecv[i].astype(jnp.float32)

    r = iota((64, BLK), 0)
    pos = iota((64, BLK), 1)
    sel = (((r & 7) < CAP) & (pos == (r >> 3) * 6 + (r & 7))).astype(jnp.float32)
    ret[:, :, :FEAT] = jnp.dot(
        sel, rows, precision=HIGH, preferred_element_type=jnp.float32
    ).reshape(EXPERTS, 8, FEAT)
    ret[:, :, FEAT:] = jnp.broadcast_to(scs[...][None], (EXPERTS, 8, 128))
    for i in range(1, 8):
        e = lax.rem(own + i, 8)
        start(copy(ret.at[e], back.at[own], t_ss.at[i], t_rs.at[i], at_expert(e)))
    @pl.when(lax.rem(z, 2) == 0)
    def _():
        back[own] = ret[own]

    @pl.when(lax.rem(z, 2) == 1)
    def _():
        copy(ret.at[own], back.at[own], t_ss.at[0], t_rs.at[0], sibling).start()

    r = iota((64, TOK), 0)
    hits = []
    weight = jnp.zeros((64, TOK), jnp.float32)
    for k in range(2):
        hit = (ids[k : k + 1, :] == (r >> 3)) & (slots[k : k + 1, :] == (r & 7))
        hits.append(hit)
        weight = weight + jnp.where(hit, gates[k : k + 1, :], 0.0)
    for i in range(1, 8):
        j = lax.rem(own + 8 - i, 8)
        copy(ret.at[j], back.at[j], t_ss.at[i], t_rs.at[i], at_expert(j)).wait_recv()

    @pl.when(lax.rem(z, 2) == 1)
    def _():
        copy(ret.at[own], back.at[own], t_ss.at[0], t_rs.at[0], sibling).wait()

    d_tok[...] = lax.dot_general(
        weight, back[:, :, :FEAT].reshape(64, FEAT), (((0,), (0,)), ((), ())),
        precision=HIGH, preferred_element_type=jnp.float32,
    ).astype(jnp.bfloat16)
    sc = back[:, :, FEAT:]
    same = lax.rem(iota((EXPERTS, 8, 128), 0) + own, 2) == 0
    row = jnp.where(same, yl, 3 - yl)
    sc = jnp.sum(jnp.where(iota((EXPERTS, 8, 128), 1) == row, sc, 0.0), axis=1, keepdims=True)
    sc = jnp.broadcast_to(sc, (EXPERTS, 8, 128)).reshape(64, 128)
    lane = own * 8 + (iota((64, 128), 0) & 7)
    sc = jnp.sum(jnp.where(iota((64, 128), 1) == lane, sc, 0.0), axis=1, keepdims=True)
    for k in range(2):
        d_gate[k : k + 1, :] = jnp.sum(jnp.where(hits[k], sc, 0.0), axis=0, keepdims=True)
    for cp in waits:
        cp.wait_send()


def local(tokens_in, d_out, gates, expert_ids, slot_ids, w_gate, w_up, w_down):
    vmem = pl.BlockSpec(memory_space=pltpu.VMEM)
    hbm = pl.BlockSpec(memory_space=pltpu.HBM)
    bf, f32, dma = jnp.bfloat16, jnp.float32, pltpu.SemaphoreType.DMA
    scratch = [
        pltpu.VMEM((TOK, FEAT), bf),
        pltpu.VMEM((TOK, FEAT), bf),
        pltpu.VMEM((2, TOK), f32),
        pltpu.VMEM((2, TOK), jnp.int32),
        pltpu.VMEM((2, TOK), jnp.int32),
        pltpu.VMEM((NZ * FEAT, 4 * HID), bf),
        pltpu.VMEM((2 * HID, NZ * FEAT), bf),
        pltpu.VMEM((EXPERTS, 16, FEAT), bf),
        pltpu.VMEM((EXPERTS, 16, FEAT), bf),
        pltpu.VMEM((NZ, 2, HALF, FEAT), bf),
        pltpu.VMEM((HALF, 4 * HID), f32),
        pltpu.VMEM((HALF, 2 * HID), f32),
        pltpu.VMEM((HALF, 4 * HID), bf),
        pltpu.VMEM((NZ, HALF, FEAT), f32),
        pltpu.VMEM((4, HALF, FEAT), bf),
        pltpu.VMEM((4, HALF, FEAT), bf),
        pltpu.VMEM((4, HALF, FEAT), bf),
        pltpu.VMEM((4, HALF, FEAT), bf),
        pltpu.VMEM((HALF, FEAT), f32),
        pltpu.VMEM((4, BLK, FEAT), bf),
        pltpu.VMEM((4, BLK, FEAT), bf),
        pltpu.VMEM((EXPERTS, 8, FEAT + 128), f32),
        pltpu.VMEM((EXPERTS, 8, FEAT + 128), f32),
        pltpu.VMEM((NZ, 8, 128), f32),
        pltpu.VMEM((4, 8, 128), f32),
        pltpu.VMEM((8, 128), f32),
        dma((5,)), dma((3,)),
        dma((3,)), dma((3,)),
        dma((8,)), dma((8,)),
        dma((4,)), dma((4,)),
        dma((8, 4)), dma((8, 4)),
        dma((8,)), dma((8,)),
        dma((4, 2)), dma((4, 2)),
        dma((4, 2)), dma((4, 2)),
        dma((4, 2)), dma((4, 2)),
        dma((4, 2)), dma((4, 2)),
        dma((4, 2)), dma((4, 2)),
        dma((8,)), dma((8,)),
        dma((8,)), dma((8,)),
        dma((4,)), dma((4,)),
    ]
    d_tok, d_gate = pl.pallas_call(
        kernel,
        out_shape=(
            jax.ShapeDtypeStruct((TOK, FEAT), bf),
            jax.ShapeDtypeStruct((2, TOK), f32),
        ),
        in_specs=[hbm] * 8,
        out_specs=(vmem, vmem),
        scratch_shapes=scratch,
        name="moe_dx",
        compiler_params=pltpu.CompilerParams(
            collective_id=0, has_side_effects=True, vmem_limit_bytes=60 * 2**20
        ),
        cost_estimate=pl.CostEstimate(
            flops=5 * 2 * HALF * NZ * FEAT * 2 * HID, bytes_accessed=6 * NZ * FEAT * HID, transcendentals=HALF * 2 * HID
        ),
    )(tokens_in, d_out, gates.T, expert_ids.T, slot_ids.T, w_gate, w_up, w_down)
    return d_tok, d_gate.T


def solution(mesh):
    placed = (
        P("ep", "tp"),
        P("ep", "tp"),
        P("ep", None),
        P("ep", None),
        P("ep", None),
        P(None, ("ep", "tp")),
        P(None, ("ep", "tp")),
        P(("ep", "tp"), None),
    )
    return jax.shard_map(
        local, mesh=mesh, in_specs=placed, out_specs=(P("ep", "tp"), P("ep", None)), check_vma=False
    )
```

```python
import jax
import jax.numpy as jnp
from jax import lax
from jax.experimental import pallas as pl
from jax.experimental.pallas import tpu as pltpu
from jax.sharding import PartitionSpec as P

MESH = pl.DeviceIdType.MESH
HIGH = lax.Precision.HIGHEST
EXPERTS = 8
CAP = 6
TOK = 16
NZ = 8
FEAT = 384
HID = 256
BLK = 48
HALF = 192
PR = 32
QR = BLK - PR
PALL = 4 * PR


def iota(shape, dim):
    return lax.broadcasted_iota(jnp.int32, shape, dim)


def div6(v):
    return (v * 43) >> 8


def row_of(r):
    q = r - PALL
    first = r < PALL
    return jnp.where(first, r >> 5, q >> 4), jnp.where(first, r & (PR - 1), PR + (q & (QR - 1)))


def kernel(
    tok_h, dout_h, gates_h, ids_h, slots_h, wg, wu, wd, d_tok, d_gate,
    tok, dout, gates, ids, slots, wgu, wdn, send, drecv, G, acc_gu, acc_b, gcat, part,
    rsend, rrecv, lsend, lrecv, total, ysend, yrecv, ret, back, scz, scy, scs,
    i_sem, w_sem, p_ss, p_rs, d_ss, d_rs, y_ss, y_rs, q_ss, q_rs, qz_ss, qz_rs, r_ss, r_rs, l_ss, l_rs,
    rr_ss, rr_rs, rl_ss, rl_rs, yy_ss, yy_rs, t_ss, t_rs, z_ss, z_rs, s_ss, s_rs,
):
    ep = lax.axis_index("ep")
    z = lax.axis_index("tp")
    own = lax.div(ep, 8)
    place = lax.rem(ep, 8)
    yl = lax.div(place, 2)
    c = lax.rem(place, 2)

    def at_expert(e):
        mirrored = lax.rem(own + e, 2)
        return (e * 8 + (yl + mirrored * (3 - 2 * yl)) * 2 + lax.rem(c + z, 2), z)

    def at_y(yy):
        return (own * 8 + yy * 2 + c, z)

    def at_z(zz):
        return (own * 8 + yl * 2 + lax.rem(c + z + zz, 2), zz)

    sibling = (own * 8 + yl * 2 + 1 - c, z)

    def copy(src, dst, ss, rs, dev):
        return pltpu.make_async_remote_copy(
            src_ref=src, dst_ref=dst, send_sem=ss, recv_sem=rs, device_id=dev, device_id_type=MESH
        )

    waits = []

    def start(cp):
        cp.start()
        waits.append(cp)

    def weights(core):
        at = pl.multiple_of(core * HID, HID)
        return (
            (wg, wgu.at[:, pl.ds(at, HID)]),
            (wu, wgu.at[:, pl.ds(pl.multiple_of(at + 2 * HID, HID), HID)]),
            (wd, wdn.at[pl.ds(at, HID), :]),
        )

    small = [
        pltpu.make_async_copy(src, dst, i_sem.at[i])
        for i, (src, dst) in enumerate(
            ((ids_h, ids), (slots_h, slots), (tok_h, tok), (dout_h, dout), (gates_h, gates))
        )
    ]
    loads = [
        pltpu.make_async_copy(src, dst, w_sem.at[i]) for i, (src, dst) in enumerate(weights(c))
    ]
    for ld in small + loads:
        ld.start()

    barrier = pltpu.get_barrier_semaphore()
    peers = [at_expert(lax.rem(own + i, 8)) for i in range(1, 8)]
    peers += [at_y(lax.rem(yl + i, 4)) for i in range(1, 4)]
    peers += [at_z(lax.rem(z + i, NZ)) for i in range(1, NZ)]
    peers += [sibling]
    for dev in peers:
        pl.semaphore_signal(barrier, inc=1, device_id=dev, device_id_type=MESH)

    for ld in small:
        ld.wait()
    r = iota((128, TOK), 0)
    pick = jnp.zeros((128, TOK), jnp.float32)
    for k in range(2):
        hit = (ids[k : k + 1, :] == (r >> 4)) & (slots[k : k + 1, :] == (r & 7))
        pick = pick + hit.astype(jnp.float32)
    is_back = (r & 8) == 8
    pick_in = jnp.where(is_back, 0.0, pick).astype(jnp.bfloat16)
    pick_back = jnp.where(is_back, pick, 0.0).astype(jnp.bfloat16)
    placed = jnp.dot(pick_in, tok[...], preferred_element_type=jnp.float32)
    placed = placed + jnp.dot(pick_back, dout[...], preferred_element_type=jnp.float32)
    send[...] = placed.astype(jnp.bfloat16).reshape(EXPERTS, 16, FEAT)

    pl.semaphore_wait(barrier, len(peers))

    for i in range(1, 8):
        e = lax.rem(own + i, 8)
        start(copy(send.at[e], drecv.at[own], d_ss.at[i], d_rs.at[i], at_expert(e)))
    for i, (src, dst) in enumerate(weights(c)):
        start(copy(src, dst, p_ss.at[i], p_rs.at[i], sibling))
    @pl.when(lax.rem(z, 2) == 0)
    def _():
        drecv[own] = send[own]

    @pl.when(lax.rem(z, 2) == 1)
    def _():
        copy(send.at[own], drecv.at[own], d_ss.at[0], d_rs.at[0], sibling).start()

    r = iota((2 * BLK, 128), 0)
    second = (r >= BLK).astype(jnp.int32)
    q = r - second * BLK
    j6 = div6(q)
    sel = (iota((2 * BLK, 128), 1) == j6 * 16 + second * 8 + (q - 6 * j6)).astype(jnp.bfloat16)
    for i in range(1, 8):
        j = lax.rem(own + 8 - i, 8)
        copy(send.at[j], drecv.at[j], d_ss.at[i], d_rs.at[i], at_expert(j)).wait_recv()

    @pl.when(lax.rem(z, 2) == 1)
    def _():
        copy(send.at[own], drecv.at[own], d_ss.at[0], d_rs.at[0], sibling).wait()

    dense = jnp.dot(sel, drecv[...].reshape(128, FEAT), preferred_element_type=jnp.float32)
    dense = dense.astype(jnp.bfloat16)
    p_rows = pl.ds(pl.multiple_of(yl * PR, PR), PR)
    q_rows = pl.ds(pl.multiple_of(PALL + yl * QR, QR), QR)
    for a in range(2):
        G[z, a, p_rows, :] = dense[a * BLK : a * BLK + PR]
        G[z, a, q_rows, :] = dense[a * BLK + PR : (a + 1) * BLK]

    def slot_of(n):
        if n == 0:
            return z
        if n <= 3:
            return lax.rem(z + NZ - n, NZ)
        if n <= 6:
            return lax.rem(z + n - 3, NZ)
        return lax.rem(z + 4, NZ)

    z_right, z_left = at_z(lax.rem(z + 1, NZ)), at_z(lax.rem(z + NZ - 1, NZ))

    def q_own(i):
        blk = G.at[z, :, q_rows]
        return copy(blk, blk, qz_ss.at[i], qz_rs.at[i], at_z(lax.rem(z + i, NZ)))

    def q_from(i):
        zz = lax.rem(z + NZ - i, NZ)
        blk = G.at[zz, :, q_rows]
        return copy(blk, blk, qz_ss.at[i], qz_rs.at[i], at_z(zz))

    def q_relay(slot, a, dev):
        blk = G.at[slot, a, q_rows]
        return copy(blk, blk, qz_ss.at[4 * a], qz_rs.at[4 * a], dev)

    def q_spread(n):
        blk = G.at[slot_of(n), :, q_rows]
        for i in range(1, 4):
            start(copy(blk, blk, q_ss.at[n, i], q_rs.at[n, i], at_y(lax.rem(yl + i, 4))))

    def q_got(n):
        for i in range(1, 4):
            yy = lax.rem(yl + 4 - i, 4)
            blk = G.at[slot_of(n), :, pl.ds(pl.multiple_of(PALL + yy * QR, QR), QR)]
            copy(blk, blk, q_ss.at[n, i], q_rs.at[n, i], at_y(yy)).wait_recv()

    def over_y(i, yy, dev):
        blk = G.at[z, :, pl.ds(pl.multiple_of(yy * PR, PR), PR)]
        return copy(blk, blk, y_ss.at[i], y_rs.at[i], dev)

    def right(k, a, shift=0):
        blk = G.at[lax.rem(z + NZ - k - shift, NZ), a, pl.ds(0, PALL)]
        return copy(blk, blk, r_ss.at[k, a], r_rs.at[k, a], z_right)

    def left(k, a, shift=0):
        blk = G.at[lax.rem(z + k + shift, NZ), a, pl.ds(0, PALL)]
        return copy(blk, blk, l_ss.at[k, a], l_rs.at[k, a], z_left)

    def p_step(k):
        for a in range(2):
            if k < 3 or a == 0:
                right(k, a, 1).wait_recv()
                if k < 2 or (k == 2 and a == 0):
                    start(right(k + 1, a))
            if k < 3 or a == 1:
                left(k, a, 1).wait_recv()
                if k < 2 or (k == 2 and a == 1):
                    start(left(k + 1, a))

    def products(n):
        q_got(n)
        slot = slot_of(n)
        base = pl.multiple_of(slot * FEAT, FEAT)
        acc_gu[...] += jnp.dot(
            G[slot, 0], wgu[pl.ds(base, FEAT), :], preferred_element_type=jnp.float32
        )
        acc_b[...] += lax.dot_general(
            G[slot, 1], wdn[:, pl.ds(base, FEAT)], (((1,), (1,)), ((), ())),
            preferred_element_type=jnp.float32,
        )

    near = (1, 7, 2, 6, 3, 5)
    for i in near:
        start(q_own(i))
    for i in range(1, 4):
        yy = lax.rem(yl + i, 4)
        start(over_y(i, yl, at_y(yy)))
    q_spread(0)
    acc_gu[...] = jnp.zeros_like(acc_gu)
    acc_b[...] = jnp.zeros_like(acc_b)
    ret[...] = jnp.zeros_like(ret)
    for i in range(1, 4):
        yy = lax.rem(yl + 4 - i, 4)
        over_y(i, yy, at_y(yy)).wait_recv()
    for a in range(2):
        start(right(0, a))
        start(left(0, a))
    for i in near:
        if i == 3:
            p_step(0)
        q_from(i).wait_recv()
        if i == 3:
            start(q_relay(lax.rem(z + NZ - 3, NZ), 0, z_right))
        if i == 5:
            start(q_relay(lax.rem(z + 3, NZ), 1, z_left))
        q_spread(i if i <= 3 else 11 - i)
    for ld in loads:
        ld.wait()
    for i, (src, dst) in enumerate(weights(1 - c)):
        copy(src, dst, p_ss.at[i], p_rs.at[i], sibling).wait_recv()
    products(0)
    q_relay(slot_of(7), 0, z_right).wait_recv()
    q_relay(slot_of(7), 1, z_left).wait_recv()
    q_spread(7)
    p_step(1)
    products(1)
    products(4)
    p_step(2)
    products(2)
    products(5)
    products(3)
    products(6)
    p_step(3)
    products(7)

    parts = (pl.ds(0, PALL), pl.ds(PALL, HALF - PALL))

    def hidden(h):
        gate = acc_gu[parts[h], : 2 * HID]
        up = acc_gu[parts[h], 2 * HID :]
        bg = acc_b[parts[h], :]
        sg = jax.nn.sigmoid(gate)
        silu = gate * sg
        gcat[parts[h], : 2 * HID] = (bg * up * sg * (1.0 + gate * (1.0 - sg))).astype(jnp.bfloat16)
        gcat[parts[h], 2 * HID :] = (bg * silu).astype(jnp.bfloat16)
        return jnp.sum(silu * up * bg, axis=1, keepdims=True)

    def slice_grad(slot, rows):
        base = pl.multiple_of(slot * FEAT, FEAT)
        part[slot, rows, :] = lax.dot_general(
            gcat[rows, :], wgu[pl.ds(base, FEAT), :], (((1,), (1,)), ((), ())),
            preferred_element_type=jnp.float32,
        )

    def ring_r(k, h):
        return copy(
            rsend.at[k, parts[h]], rrecv.at[k, parts[h]], rr_ss.at[k, h], rr_rs.at[k, h], z_right
        )

    def ring_l(k, h):
        return copy(
            lsend.at[k, parts[h]], lrecv.at[k, parts[h]], rl_ss.at[k, h], rl_rs.at[k, h], z_left
        )

    far = slot_of(7)
    score0 = hidden(0)
    slice_grad(far, parts[0])
    rsend[0, parts[0], :] = part[far, parts[0], :].astype(jnp.bfloat16)
    start(ring_r(0, 0))
    score1 = hidden(1)
    slice_grad(far, parts[1])
    lsend[0, parts[1], :] = part[far, parts[1], :].astype(jnp.bfloat16)
    start(ring_l(0, 1))
    score = jnp.concatenate([score0, score1], axis=0)

    q = row_of(iota((HALF, 128), 0))[1]
    j6 = div6(q)
    spread = jnp.where(iota((HALF, 128), 1) == j6 * 8 + (q - 6 * j6), score, 0.0)
    mine = (row_of(iota((8, HALF), 1))[0] == iota((8, HALF), 0)).astype(jnp.float32)
    scz[z] = jnp.dot(mine, spread, precision=HIGH, preferred_element_type=jnp.float32)
    for i in range(1, NZ):
        start(copy(scz.at[z], scz.at[z], z_ss.at[i], z_rs.at[i], at_z(lax.rem(z + i, NZ))))

    for k in range(1, 4):
        nr, nl = slot_of(7 - k), slot_of(4 - k)
        slice_grad(nr, pl.ds(0, HALF))
        slice_grad(nl, pl.ds(0, HALF))
        for h, ring, slot, out, got in (
            (1, ring_r, nr, rsend, rrecv),
            (0, ring_l, nl, lsend, lrecv),
            (0, ring_r, nr, rsend, rrecv),
            (1, ring_l, nl, lsend, lrecv),
        ):
            term = part[slot, parts[h], :]
            if k > 1 or (h == 0) == (out is rsend):
                ring(k - 1, h).wait_recv()
                term = term + got[k - 1, parts[h], :].astype(jnp.float32)
            out[k, parts[h], :] = term.astype(jnp.bfloat16)
            start(ring(k, h))
        if k == 2:
            for i in range(1, NZ):
                zz = lax.rem(z + NZ - i, NZ)
                copy(scz.at[zz], scz.at[zz], z_ss.at[i], z_rs.at[i], at_z(zz)).wait_recv()
            scy[yl] = jnp.sum(scz[...], axis=0)
            for i in range(1, 4):
                yy = lax.rem(yl + i, 4)
                start(copy(scy.at[yl], scy.at[yl], s_ss.at[i], s_rs.at[i], at_y(yy)))
    slice_grad(z, pl.ds(0, HALF))
    for i in range(1, 4):
        yy = lax.rem(yl + 4 - i, 4)
        copy(scy.at[yy], scy.at[yy], s_ss.at[i], s_rs.at[i], at_y(yy)).wait_recv()
    scs[...] = jnp.sum(scy[...], axis=0)
    places = (pl.ds(0, PR), pl.ds(PR, QR))
    for h, size in ((1, QR), (0, PR)):
        ring_r(3, h).wait_recv()
        ring_l(3, h).wait_recv()
        summed = part[z, parts[h], :] + rrecv[3, parts[h], :].astype(jnp.float32)
        summed = summed + lrecv[3, parts[h], :].astype(jnp.float32)
        total[parts[h], :] = summed
        ysend[:, places[h], :] = summed.astype(jnp.bfloat16).reshape(4, size, FEAT)
        for i in range(1, 4):
            yy = lax.rem(yl + i, 4)
            start(
                copy(
                    ysend.at[yy, places[h]], yrecv.at[i, places[h]],
                    yy_ss.at[i, h], yy_rs.at[i, h], at_y(yy),
                )
            )
    rows = jnp.concatenate([total[p_rows, :], total[q_rows, :]], axis=0)
    for i in range(1, 4):
        for h in (1, 0):
            dst = yrecv.at[i, places[h]]
            copy(dst, dst, yy_ss.at[i, h], yy_rs.at[i, h], at_y(lax.rem(yl + 4 - i, 4))).wait_recv()
        rows = rows + yrecv[i].astype(jnp.float32)

    for j in range(EXPERTS):
        ret[j, :CAP, :FEAT] = rows[j * CAP : (j + 1) * CAP]
    ret[:, :, FEAT:] = jnp.broadcast_to(scs[...][None], (EXPERTS, 8, 128))
    for i in range(1, 8):
        e = lax.rem(own + i, 8)
        start(copy(ret.at[e], back.at[own], t_ss.at[i], t_rs.at[i], at_expert(e)))
    @pl.when(lax.rem(z, 2) == 0)
    def _():
        back[own] = ret[own]

    @pl.when(lax.rem(z, 2) == 1)
    def _():
        copy(ret.at[own], back.at[own], t_ss.at[0], t_rs.at[0], sibling).start()

    r = iota((64, TOK), 0)
    hits = []
    weight = jnp.zeros((64, TOK), jnp.float32)
    for k in range(2):
        hit = (ids[k : k + 1, :] == (r >> 3)) & (slots[k : k + 1, :] == (r & 7))
        hits.append(hit)
        weight = weight + jnp.where(hit, gates[k : k + 1, :], 0.0)
    for i in range(1, 8):
        j = lax.rem(own + 8 - i, 8)
        copy(ret.at[j], back.at[j], t_ss.at[i], t_rs.at[i], at_expert(j)).wait_recv()

    @pl.when(lax.rem(z, 2) == 1)
    def _():
        copy(ret.at[own], back.at[own], t_ss.at[0], t_rs.at[0], sibling).wait()

    d_tok[...] = lax.dot_general(
        weight, back[:, :, :FEAT].reshape(64, FEAT), (((0,), (0,)), ((), ())),
        precision=HIGH, preferred_element_type=jnp.float32,
    ).astype(jnp.bfloat16)
    sc = back[:, :, FEAT:]
    same = lax.rem(iota((EXPERTS, 8, 128), 0) + own, 2) == 0
    row = jnp.where(same, yl, 3 - yl)
    sc = jnp.sum(jnp.where(iota((EXPERTS, 8, 128), 1) == row, sc, 0.0), axis=1, keepdims=True)
    sc = jnp.broadcast_to(sc, (EXPERTS, 8, 128)).reshape(64, 128)
    lane = own * 8 + (iota((64, 128), 0) & 7)
    sc = jnp.sum(jnp.where(iota((64, 128), 1) == lane, sc, 0.0), axis=1, keepdims=True)
    for k in range(2):
        d_gate[k : k + 1, :] = jnp.sum(jnp.where(hits[k], sc, 0.0), axis=0, keepdims=True)
    for cp in waits:
        cp.wait_send()


def local(tokens_in, d_out, gates, expert_ids, slot_ids, w_gate, w_up, w_down):
    vmem = pl.BlockSpec(memory_space=pltpu.VMEM)
    hbm = pl.BlockSpec(memory_space=pltpu.HBM)
    bf, f32, dma = jnp.bfloat16, jnp.float32, pltpu.SemaphoreType.DMA
    scratch = [
        pltpu.VMEM((TOK, FEAT), bf),
        pltpu.VMEM((TOK, FEAT), bf),
        pltpu.VMEM((2, TOK), f32),
        pltpu.VMEM((2, TOK), jnp.int32),
        pltpu.VMEM((2, TOK), jnp.int32),
        pltpu.VMEM((NZ * FEAT, 4 * HID), bf),
        pltpu.VMEM((2 * HID, NZ * FEAT), bf),
        pltpu.VMEM((EXPERTS, 16, FEAT), bf),
        pltpu.VMEM((EXPERTS, 16, FEAT), bf),
        pltpu.VMEM((NZ, 2, HALF, FEAT), bf),
        pltpu.VMEM((HALF, 4 * HID), f32),
        pltpu.VMEM((HALF, 2 * HID), f32),
        pltpu.VMEM((HALF, 4 * HID), bf),
        pltpu.VMEM((NZ, HALF, FEAT), f32),
        pltpu.VMEM((4, HALF, FEAT), bf),
        pltpu.VMEM((4, HALF, FEAT), bf),
        pltpu.VMEM((4, HALF, FEAT), bf),
        pltpu.VMEM((4, HALF, FEAT), bf),
        pltpu.VMEM((HALF, FEAT), f32),
        pltpu.VMEM((4, BLK, FEAT), bf),
        pltpu.VMEM((4, BLK, FEAT), bf),
        pltpu.VMEM((EXPERTS, 8, FEAT + 128), f32),
        pltpu.VMEM((EXPERTS, 8, FEAT + 128), f32),
        pltpu.VMEM((NZ, 8, 128), f32),
        pltpu.VMEM((4, 8, 128), f32),
        pltpu.VMEM((8, 128), f32),
        dma((5,)), dma((3,)),
        dma((3,)), dma((3,)),
        dma((8,)), dma((8,)),
        dma((4,)), dma((4,)),
        dma((8, 4)), dma((8, 4)),
        dma((8,)), dma((8,)),
        dma((4, 2)), dma((4, 2)),
        dma((4, 2)), dma((4, 2)),
        dma((4, 2)), dma((4, 2)),
        dma((4, 2)), dma((4, 2)),
        dma((4, 2)), dma((4, 2)),
        dma((8,)), dma((8,)),
        dma((8,)), dma((8,)),
        dma((4,)), dma((4,)),
    ]
    d_tok, d_gate = pl.pallas_call(
        kernel,
        out_shape=(
            jax.ShapeDtypeStruct((TOK, FEAT), bf),
            jax.ShapeDtypeStruct((2, TOK), f32),
        ),
        in_specs=[hbm] * 8,
        out_specs=(vmem, vmem),
        scratch_shapes=scratch,
        name="moe_dx",
        compiler_params=pltpu.CompilerParams(
            collective_id=0, has_side_effects=True, vmem_limit_bytes=60 * 2**20
        ),
        cost_estimate=pl.CostEstimate(
            flops=5 * 2 * HALF * NZ * FEAT * 2 * HID, bytes_accessed=6 * NZ * FEAT * HID, transcendentals=HALF * 2 * HID
        ),
    )(tokens_in, d_out, gates.T, expert_ids.T, slot_ids.T, w_gate, w_up, w_down)
    return d_tok, d_gate.T


def solution(mesh):
    placed = (
        P("ep", "tp"),
        P("ep", "tp"),
        P("ep", None),
        P("ep", None),
        P("ep", None),
        P(None, ("ep", "tp")),
        P(None, ("ep", "tp")),
        P(("ep", "tp"), None),
    )
    return jax.shard_map(
        local, mesh=mesh, in_specs=placed, out_specs=(P("ep", "tp"), P("ep", None)), check_vma=False
    )
```

```python
import jax
import jax.numpy as jnp
from jax import lax
from jax.experimental import pallas as pl
from jax.experimental.pallas import tpu as pltpu
from jax.sharding import PartitionSpec as P

MESH = pl.DeviceIdType.MESH
HIGH = lax.Precision.HIGHEST
EXPERTS = 8
CAP = 6
TOK = 16
NZ = 8
FEAT = 384
HID = 256
BLK = 48
HALF = 192
PR = 32
QR = BLK - PR
PALL = 4 * PR


def iota(shape, dim):
    return lax.broadcasted_iota(jnp.int32, shape, dim)


def div6(v):
    return (v * 43) >> 8


def row_of(r):
    q = r - PALL
    first = r < PALL
    return jnp.where(first, r >> 5, q >> 4), jnp.where(first, r & (PR - 1), PR + (q & (QR - 1)))


def kernel(
    tok_h, dout_h, gates_h, ids_h, slots_h, wg, wu, wd, d_tok, d_gate,
    tok, dout, gates, ids, slots, wgu, wdn, send, drecv, G, acc_gu, acc_b, gcat, part,
    rsend, rrecv, lsend, lrecv, total, ysend, yrecv, ret, back, scz, scy, scs,
    i_sem, w_sem, p_ss, p_rs, d_ss, d_rs, y_ss, y_rs, q_ss, q_rs, qz_ss, qz_rs, r_ss, r_rs, l_ss, l_rs,
    rr_ss, rr_rs, rl_ss, rl_rs, yy_ss, yy_rs, t_ss, t_rs, z_ss, z_rs, s_ss, s_rs,
):
    ep = lax.axis_index("ep")
    z = lax.axis_index("tp")
    own = lax.div(ep, 8)
    place = lax.rem(ep, 8)
    yl = lax.div(place, 2)
    c = lax.rem(place, 2)

    def at_expert(e):
        mirrored = lax.rem(own + e, 2)
        return (e * 8 + (yl + mirrored * (3 - 2 * yl)) * 2 + lax.rem(c + z, 2), z)

    def at_y(yy):
        return (own * 8 + yy * 2 + c, z)

    def at_z(zz):
        return (own * 8 + yl * 2 + lax.rem(c + z + zz, 2), zz)

    sibling = (own * 8 + yl * 2 + 1 - c, z)

    def copy(src, dst, ss, rs, dev):
        return pltpu.make_async_remote_copy(
            src_ref=src, dst_ref=dst, send_sem=ss, recv_sem=rs, device_id=dev, device_id_type=MESH
        )

    waits = []

    def start(cp):
        cp.start()
        waits.append(cp)

    def weights(core):
        at = pl.multiple_of(core * HID, HID)
        return (
            (wg, wgu.at[:, pl.ds(at, HID)]),
            (wu, wgu.at[:, pl.ds(pl.multiple_of(at + 2 * HID, HID), HID)]),
            (wd, wdn.at[pl.ds(at, HID), :]),
        )

    small = [
        pltpu.make_async_copy(src, dst, i_sem.at[i])
        for i, (src, dst) in enumerate(
            ((ids_h, ids), (slots_h, slots), (tok_h, tok), (dout_h, dout), (gates_h, gates))
        )
    ]
    loads = [
        pltpu.make_async_copy(src, dst, w_sem.at[i]) for i, (src, dst) in enumerate(weights(c))
    ]
    for ld in small + loads:
        ld.start()

    barrier = pltpu.get_barrier_semaphore()
    peers = [at_expert(lax.rem(own + i, 8)) for i in range(1, 8)]
    peers += [at_y(lax.rem(yl + i, 4)) for i in range(1, 4)]
    peers += [at_z(lax.rem(z + i, NZ)) for i in range(1, NZ)]
    peers += [sibling]
    for dev in peers:
        pl.semaphore_signal(barrier, inc=1, device_id=dev, device_id_type=MESH)

    for ld in small:
        ld.wait()
    r = iota((128, TOK), 0)
    pick = jnp.zeros((128, TOK), jnp.float32)
    for k in range(2):
        hit = (ids[k : k + 1, :] == (r >> 4)) & (slots[k : k + 1, :] == (r & 7))
        pick = pick + hit.astype(jnp.float32)
    is_back = (r & 8) == 8
    pick_in = jnp.where(is_back, 0.0, pick).astype(jnp.bfloat16)
    pick_back = jnp.where(is_back, pick, 0.0).astype(jnp.bfloat16)
    placed = jnp.dot(pick_in, tok[...], preferred_element_type=jnp.float32)
    placed = placed + jnp.dot(pick_back, dout[...], preferred_element_type=jnp.float32)
    send[...] = placed.astype(jnp.bfloat16).reshape(EXPERTS, 16, FEAT)

    pl.semaphore_wait(barrier, len(peers))

    for i in range(1, 8):
        e = lax.rem(own + i, 8)
        start(copy(send.at[e], drecv.at[own], d_ss.at[i], d_rs.at[i], at_expert(e)))
    for i, (src, dst) in enumerate(weights(c)):
        start(copy(src, dst, p_ss.at[i], p_rs.at[i], sibling))
    @pl.when(lax.rem(z, 2) == 0)
    def _():
        drecv[own] = send[own]

    @pl.when(lax.rem(z, 2) == 1)
    def _():
        copy(send.at[own], drecv.at[own], d_ss.at[0], d_rs.at[0], sibling).start()

    r = iota((2 * BLK, 128), 0)
    second = (r >= BLK).astype(jnp.int32)
    q = r - second * BLK
    j6 = div6(q)
    sel = (iota((2 * BLK, 128), 1) == j6 * 16 + second * 8 + (q - 6 * j6)).astype(jnp.bfloat16)
    for i in range(1, 8):
        j = lax.rem(own + 8 - i, 8)
        copy(send.at[j], drecv.at[j], d_ss.at[i], d_rs.at[i], at_expert(j)).wait_recv()

    @pl.when(lax.rem(z, 2) == 1)
    def _():
        copy(send.at[own], drecv.at[own], d_ss.at[0], d_rs.at[0], sibling).wait()

    dense = jnp.dot(sel, drecv[...].reshape(128, FEAT), preferred_element_type=jnp.float32)
    dense = dense.astype(jnp.bfloat16)
    p_rows = pl.ds(pl.multiple_of(yl * PR, PR), PR)
    q_rows = pl.ds(pl.multiple_of(PALL + yl * QR, QR), QR)
    for a in range(2):
        G[z, a, p_rows, :] = dense[a * BLK : a * BLK + PR]
        G[z, a, q_rows, :] = dense[a * BLK + PR : (a + 1) * BLK]

    def slot_of(n):
        if n == 0:
            return z
        if n <= 3:
            return lax.rem(z + NZ - n, NZ)
        if n <= 6:
            return lax.rem(z + n - 3, NZ)
        return lax.rem(z + 4, NZ)

    z_right, z_left = at_z(lax.rem(z + 1, NZ)), at_z(lax.rem(z + NZ - 1, NZ))

    def q_own(i):
        blk = G.at[z, :, q_rows]
        return copy(blk, blk, qz_ss.at[i], qz_rs.at[i], at_z(lax.rem(z + i, NZ)))

    def q_from(i):
        zz = lax.rem(z + NZ - i, NZ)
        blk = G.at[zz, :, q_rows]
        return copy(blk, blk, qz_ss.at[i], qz_rs.at[i], at_z(zz))

    def q_spread(n):
        blk = G.at[slot_of(n), :, q_rows]
        for i in range(1, 4):
            start(copy(blk, blk, q_ss.at[n, i], q_rs.at[n, i], at_y(lax.rem(yl + i, 4))))

    def q_got(n):
        for i in range(1, 4):
            yy = lax.rem(yl + 4 - i, 4)
            blk = G.at[slot_of(n), :, pl.ds(pl.multiple_of(PALL + yy * QR, QR), QR)]
            copy(blk, blk, q_ss.at[n, i], q_rs.at[n, i], at_y(yy)).wait_recv()

    def over_y(i, yy, dev):
        blk = G.at[z, :, pl.ds(pl.multiple_of(yy * PR, PR), PR)]
        return copy(blk, blk, y_ss.at[i], y_rs.at[i], dev)

    def right(k, a, shift=0):
        blk = G.at[lax.rem(z + NZ - k - shift, NZ), a, pl.ds(0, PALL)]
        return copy(blk, blk, r_ss.at[k, a], r_rs.at[k, a], z_right)

    def left(k, a, shift=0):
        blk = G.at[lax.rem(z + k + shift, NZ), a, pl.ds(0, PALL)]
        return copy(blk, blk, l_ss.at[k, a], l_rs.at[k, a], z_left)

    def p_step(k):
        for a in range(2):
            if k < 3 or a == 0:
                right(k, a, 1).wait_recv()
                if k < 2 or (k == 2 and a == 0):
                    start(right(k + 1, a))
            if k < 3 or a == 1:
                left(k, a, 1).wait_recv()
                if k < 2 or (k == 2 and a == 1):
                    start(left(k + 1, a))

    def products(n):
        q_got(n)
        slot = slot_of(n)
        base = pl.multiple_of(slot * FEAT, FEAT)
        acc_gu[...] += jnp.dot(
            G[slot, 0], wgu[pl.ds(base, FEAT), :], preferred_element_type=jnp.float32
        )
        acc_b[...] += lax.dot_general(
            G[slot, 1], wdn[:, pl.ds(base, FEAT)], (((1,), (1,)), ((), ())),
            preferred_element_type=jnp.float32,
        )

    near = (1, 7, 2, 6, 3, 5, 4)
    for i in range(1, 4):
        yy = lax.rem(yl + i, 4)
        start(over_y(i, yl, at_y(yy)))
    for i in near[::-1]:
        start(q_own(i))
    q_spread(0)
    acc_gu[...] = jnp.zeros_like(acc_gu)
    acc_b[...] = jnp.zeros_like(acc_b)
    ret[...] = jnp.zeros_like(ret)
    for i in range(1, 4):
        yy = lax.rem(yl + 4 - i, 4)
        over_y(i, yy, at_y(yy)).wait_recv()
    for a in range(2):
        start(right(0, a))
        start(left(0, a))
    for i in near:
        q_from(i).wait_recv()
        q_spread(i if i <= 3 else 7 if i == 4 else 11 - i)
    for ld in loads:
        ld.wait()
    for i, (src, dst) in enumerate(weights(1 - c)):
        copy(src, dst, p_ss.at[i], p_rs.at[i], sibling).wait_recv()
    p_step(0)
    products(0)
    p_step(1)
    products(1)
    products(4)
    p_step(2)
    products(2)
    products(5)
    products(3)
    products(6)
    p_step(3)
    products(7)

    parts = (pl.ds(0, PALL), pl.ds(PALL, HALF - PALL))

    def hidden(h):
        gate = acc_gu[parts[h], : 2 * HID]
        up = acc_gu[parts[h], 2 * HID :]
        bg = acc_b[parts[h], :]
        sg = jax.nn.sigmoid(gate)
        silu = gate * sg
        gcat[parts[h], : 2 * HID] = (bg * up * sg * (1.0 + gate * (1.0 - sg))).astype(jnp.bfloat16)
        gcat[parts[h], 2 * HID :] = (bg * silu).astype(jnp.bfloat16)
        return jnp.sum(silu * up * bg, axis=1, keepdims=True)

    def slice_grad(slot, rows):
        base = pl.multiple_of(slot * FEAT, FEAT)
        part[slot, rows, :] = lax.dot_general(
            gcat[rows, :], wgu[pl.ds(base, FEAT), :], (((1,), (1,)), ((), ())),
            preferred_element_type=jnp.float32,
        )

    def ring_r(k, h):
        return copy(
            rsend.at[k, parts[h]], rrecv.at[k, parts[h]], rr_ss.at[k, h], rr_rs.at[k, h], z_right
        )

    def ring_l(k, h):
        return copy(
            lsend.at[k, parts[h]], lrecv.at[k, parts[h]], rl_ss.at[k, h], rl_rs.at[k, h], z_left
        )

    far = slot_of(7)
    score0 = hidden(0)
    slice_grad(far, parts[0])
    rsend[0, parts[0], :] = part[far, parts[0], :].astype(jnp.bfloat16)
    start(ring_r(0, 0))
    score1 = hidden(1)
    slice_grad(far, parts[1])
    lsend[0, parts[1], :] = part[far, parts[1], :].astype(jnp.bfloat16)
    start(ring_l(0, 1))
    score = jnp.concatenate([score0, score1], axis=0)

    q = row_of(iota((HALF, 128), 0))[1]
    j6 = div6(q)
    spread = jnp.where(iota((HALF, 128), 1) == j6 * 8 + (q - 6 * j6), score, 0.0)
    mine = (row_of(iota((8, HALF), 1))[0] == iota((8, HALF), 0)).astype(jnp.float32)
    scz[z] = jnp.dot(mine, spread, precision=HIGH, preferred_element_type=jnp.float32)
    for i in range(1, NZ):
        start(copy(scz.at[z], scz.at[z], z_ss.at[i], z_rs.at[i], at_z(lax.rem(z + i, NZ))))

    for k in range(1, 4):
        nr, nl = slot_of(7 - k), slot_of(4 - k)
        slice_grad(nr, pl.ds(0, HALF))
        slice_grad(nl, pl.ds(0, HALF))
        for h, ring, slot, out, got in (
            (1, ring_r, nr, rsend, rrecv),
            (0, ring_l, nl, lsend, lrecv),
            (0, ring_r, nr, rsend, rrecv),
            (1, ring_l, nl, lsend, lrecv),
        ):
            term = part[slot, parts[h], :]
            if k > 1 or (h == 0) == (out is rsend):
                ring(k - 1, h).wait_recv()
                term = term + got[k - 1, parts[h], :].astype(jnp.float32)
            out[k, parts[h], :] = term.astype(jnp.bfloat16)
            start(ring(k, h))
        if k == 2:
            for i in range(1, NZ):
                zz = lax.rem(z + NZ - i, NZ)
                copy(scz.at[zz], scz.at[zz], z_ss.at[i], z_rs.at[i], at_z(zz)).wait_recv()
            scy[yl] = jnp.sum(scz[...], axis=0)
            for i in range(1, 4):
                yy = lax.rem(yl + i, 4)
                start(copy(scy.at[yl], scy.at[yl], s_ss.at[i], s_rs.at[i], at_y(yy)))
    slice_grad(z, pl.ds(0, HALF))
    for i in range(1, 4):
        yy = lax.rem(yl + 4 - i, 4)
        copy(scy.at[yy], scy.at[yy], s_ss.at[i], s_rs.at[i], at_y(yy)).wait_recv()
    scs[...] = jnp.sum(scy[...], axis=0)
    places = (pl.ds(0, PR), pl.ds(PR, QR))
    for h, size in ((1, QR), (0, PR)):
        ring_r(3, h).wait_recv()
        ring_l(3, h).wait_recv()
        summed = part[z, parts[h], :] + rrecv[3, parts[h], :].astype(jnp.float32)
        summed = summed + lrecv[3, parts[h], :].astype(jnp.float32)
        total[parts[h], :] = summed
        ysend[:, places[h], :] = summed.astype(jnp.bfloat16).reshape(4, size, FEAT)
        for i in range(1, 4):
            yy = lax.rem(yl + i, 4)
            start(
                copy(
                    ysend.at[yy, places[h]], yrecv.at[i, places[h]],
                    yy_ss.at[i, h], yy_rs.at[i, h], at_y(yy),
                )
            )
    rows = jnp.concatenate([total[p_rows, :], total[q_rows, :]], axis=0)
    for i in range(1, 4):
        for h in (1, 0):
            dst = yrecv.at[i, places[h]]
            copy(dst, dst, yy_ss.at[i, h], yy_rs.at[i, h], at_y(lax.rem(yl + 4 - i, 4))).wait_recv()
        rows = rows + yrecv[i].astype(jnp.float32)

    for j in range(EXPERTS):
        ret[j, :CAP, :FEAT] = rows[j * CAP : (j + 1) * CAP]
    ret[:, :, FEAT:] = jnp.broadcast_to(scs[...][None], (EXPERTS, 8, 128))
    for i in range(1, 8):
        e = lax.rem(own + i, 8)
        start(copy(ret.at[e], back.at[own], t_ss.at[i], t_rs.at[i], at_expert(e)))
    @pl.when(lax.rem(z, 2) == 0)
    def _():
        back[own] = ret[own]

    @pl.when(lax.rem(z, 2) == 1)
    def _():
        copy(ret.at[own], back.at[own], t_ss.at[0], t_rs.at[0], sibling).start()

    r = iota((64, TOK), 0)
    hits = []
    weight = jnp.zeros((64, TOK), jnp.float32)
    for k in range(2):
        hit = (ids[k : k + 1, :] == (r >> 3)) & (slots[k : k + 1, :] == (r & 7))
        hits.append(hit)
        weight = weight + jnp.where(hit, gates[k : k + 1, :], 0.0)
    for i in range(1, 8):
        j = lax.rem(own + 8 - i, 8)
        copy(ret.at[j], back.at[j], t_ss.at[i], t_rs.at[i], at_expert(j)).wait_recv()

    @pl.when(lax.rem(z, 2) == 1)
    def _():
        copy(ret.at[own], back.at[own], t_ss.at[0], t_rs.at[0], sibling).wait()

    d_tok[...] = lax.dot_general(
        weight, back[:, :, :FEAT].reshape(64, FEAT), (((0,), (0,)), ((), ())),
        precision=HIGH, preferred_element_type=jnp.float32,
    ).astype(jnp.bfloat16)
    sc = back[:, :, FEAT:]
    same = lax.rem(iota((EXPERTS, 8, 128), 0) + own, 2) == 0
    row = jnp.where(same, yl, 3 - yl)
    sc = jnp.sum(jnp.where(iota((EXPERTS, 8, 128), 1) == row, sc, 0.0), axis=1, keepdims=True)
    sc = jnp.broadcast_to(sc, (EXPERTS, 8, 128)).reshape(64, 128)
    lane = own * 8 + (iota((64, 128), 0) & 7)
    sc = jnp.sum(jnp.where(iota((64, 128), 1) == lane, sc, 0.0), axis=1, keepdims=True)
    for k in range(2):
        d_gate[k : k + 1, :] = jnp.sum(jnp.where(hits[k], sc, 0.0), axis=0, keepdims=True)
    for cp in waits:
        cp.wait_send()


def local(tokens_in, d_out, gates, expert_ids, slot_ids, w_gate, w_up, w_down):
    vmem = pl.BlockSpec(memory_space=pltpu.VMEM)
    hbm = pl.BlockSpec(memory_space=pltpu.HBM)
    bf, f32, dma = jnp.bfloat16, jnp.float32, pltpu.SemaphoreType.DMA
    scratch = [
        pltpu.VMEM((TOK, FEAT), bf),
        pltpu.VMEM((TOK, FEAT), bf),
        pltpu.VMEM((2, TOK), f32),
        pltpu.VMEM((2, TOK), jnp.int32),
        pltpu.VMEM((2, TOK), jnp.int32),
        pltpu.VMEM((NZ * FEAT, 4 * HID), bf),
        pltpu.VMEM((2 * HID, NZ * FEAT), bf),
        pltpu.VMEM((EXPERTS, 16, FEAT), bf),
        pltpu.VMEM((EXPERTS, 16, FEAT), bf),
        pltpu.VMEM((NZ, 2, HALF, FEAT), bf),
        pltpu.VMEM((HALF, 4 * HID), f32),
        pltpu.VMEM((HALF, 2 * HID), f32),
        pltpu.VMEM((HALF, 4 * HID), bf),
        pltpu.VMEM((NZ, HALF, FEAT), f32),
        pltpu.VMEM((4, HALF, FEAT), bf),
        pltpu.VMEM((4, HALF, FEAT), bf),
        pltpu.VMEM((4, HALF, FEAT), bf),
        pltpu.VMEM((4, HALF, FEAT), bf),
        pltpu.VMEM((HALF, FEAT), f32),
        pltpu.VMEM((4, BLK, FEAT), bf),
        pltpu.VMEM((4, BLK, FEAT), bf),
        pltpu.VMEM((EXPERTS, 8, FEAT + 128), f32),
        pltpu.VMEM((EXPERTS, 8, FEAT + 128), f32),
        pltpu.VMEM((NZ, 8, 128), f32),
        pltpu.VMEM((4, 8, 128), f32),
        pltpu.VMEM((8, 128), f32),
        dma((5,)), dma((3,)),
        dma((3,)), dma((3,)),
        dma((8,)), dma((8,)),
        dma((4,)), dma((4,)),
        dma((8, 4)), dma((8, 4)),
        dma((8,)), dma((8,)),
        dma((4, 2)), dma((4, 2)),
        dma((4, 2)), dma((4, 2)),
        dma((4, 2)), dma((4, 2)),
        dma((4, 2)), dma((4, 2)),
        dma((4, 2)), dma((4, 2)),
        dma((8,)), dma((8,)),
        dma((8,)), dma((8,)),
        dma((4,)), dma((4,)),
    ]
    d_tok, d_gate = pl.pallas_call(
        kernel,
        out_shape=(
            jax.ShapeDtypeStruct((TOK, FEAT), bf),
            jax.ShapeDtypeStruct((2, TOK), f32),
        ),
        in_specs=[hbm] * 8,
        out_specs=(vmem, vmem),
        scratch_shapes=scratch,
        name="moe_dx",
        compiler_params=pltpu.CompilerParams(
            collective_id=0, has_side_effects=True, vmem_limit_bytes=60 * 2**20
        ),
        cost_estimate=pl.CostEstimate(
            flops=5 * 2 * HALF * NZ * FEAT * 2 * HID, bytes_accessed=6 * NZ * FEAT * HID, transcendentals=HALF * 2 * HID
        ),
    )(tokens_in, d_out, gates.T, expert_ids.T, slot_ids.T, w_gate, w_up, w_down)
    return d_tok, d_gate.T


def solution(mesh):
    placed = (
        P("ep", "tp"),
        P("ep", "tp"),
        P("ep", None),
        P("ep", None),
        P("ep", None),
        P(None, ("ep", "tp")),
        P(None, ("ep", "tp")),
        P(("ep", "tp"), None),
    )
    return jax.shard_map(
        local, mesh=mesh, in_specs=placed, out_specs=(P("ep", "tp"), P("ep", None)), check_vma=False
    )
```
